256 devices in a mesh: row: 8 (over z_lo, y), col: 32 (over z_hi, x, core).
Axes of the slice: x: 4, y: 4, z: 8 (z_hi: 4, z_lo: 2; z = z_hi * 2 + z_lo), core: 2. Of those that a mesh axis runs over, the one named last changes fastest.
Arguments:
- tokens: bfloat16 [512, 12288], P('col', 'row'), may hold values from -6 to 6
- grad_out: bfloat16 [512, 12288], P('col', 'row'), may hold values from -6 to 6
- weight_in: bfloat16 [12288, 24576], P('row', 'col'), may hold values from -0.0546875 to 0.0546875
- weight_out: bfloat16 [24576, 12288], P('col', 'row'), may hold values from -0.0390625 to 0.0390625
Outputs:
- output: bfloat16 [512, 12288], P('col', 'row')
- grad_in: bfloat16 [512, 12288], P('col', 'row')
- grad_w_in: bfloat16 [12288, 24576], P('row', 'col')
- grad_w_out: bfloat16 [24576, 12288], P('col', 'row')
The draws below stay inside these ranges and needn't reach their ends.
All inputs are finite; a program needn't handle non-finite values.
Results may differ from the reference program's by a relative error of at most 0.02.
Values may be sent and summed in bfloat16 or wider, within the bound.
A program may use at most 64 MiB of HBM per device.

```python
import math
import jax
import jax.numpy as jnp

D = 12288
HID = 24576
TOKENS = 512


def shard_levels(own_key, extent, cuts, least, largest):
    def one(dim, shards_of):
        draws = jax.random.uniform(jax.random.fold_in(jax.random.fold_in(own_key, 6), dim), (shards_of,), jnp.float32, least / len(cuts), largest / len(cuts))
        return jnp.repeat(jnp.exp(draws), extent[dim] // shards_of).reshape((-1,) + (1,) * (len(extent) - dim - 1))

    loudness = one(*cuts[0])
    for cut in cuts[1:]:
        loudness = loudness * one(*cut)
    return loudness


def centred(key, extent, width, reach, shards=(), kind=jnp.bfloat16):
    result = jax.random.normal(key, extent, jnp.float32) * width
    if len(shards) > 0:
        result = shard_levels(key, extent, shards, -0.22, 0.18) * result
    return jnp.clip(result, min=-reach, max=reach).astype(kind)


def setup_inputs(seed: int = 0) -> dict:
    splits = jax.random.split(jax.random.key(seed), 5)
    tokens = centred(splits[0], (TOKENS, D), 1.0, 6.0, ((0, 32), (1, 8)))
    grad_out = centred(splits[1], (TOKENS, D), 1.0, 6.0, ((0, 32), (1, 8)))
    weight_in = centred(splits[2], (D, HID), D ** -0.5, 0.0546875, ((0, 8), (1, 32)))
    weight_out = centred(splits[3], (HID, D), HID ** -0.5, 0.0390625, ((0, 32), (1, 8)))
    return {"tokens": tokens, "grad_out": grad_out, "weight_in": weight_in, "weight_out": weight_out}


root_two_pi = math.sqrt(2.0 / math.pi)

def gelu_value(pre):
    inner = root_two_pi * (pre + 0.044715 * pre * pre * pre)
    return 0.5 * pre * (1.0 + jnp.tanh(inner))

def gelu_slope(pre):
    inner = root_two_pi * (pre + 0.044715 * pre * pre * pre)
    bent = jnp.tanh(inner)
    return 0.5 * (1.0 + bent) + 0.5 * pre * (1.0 - bent * bent) * root_two_pi * (1.0 + 3.0 * 0.044715 * pre * pre)

def reference(tokens, grad_out, weight_in, weight_out):
    hidden_pre = jnp.dot(tokens, weight_in, preferred_element_type=jnp.float32)
    hidden_grad = jnp.dot(grad_out, weight_out.T, preferred_element_type=jnp.float32)
    hidden_act = gelu_value(hidden_pre).astype(jnp.bfloat16)
    pre_grad = (hidden_grad * gelu_slope(hidden_pre)).astype(jnp.bfloat16)
    output = jnp.dot(hidden_act, weight_out, preferred_element_type=jnp.float32).astype(jnp.bfloat16)
    grad_in = jnp.dot(pre_grad, weight_in.T, preferred_element_type=jnp.float32).astype(jnp.bfloat16)
    factor = 1.0 / math.sqrt(TOKENS)
    grad_w_in = (jnp.dot(tokens.T, pre_grad, preferred_element_type=jnp.float32) * factor).astype(jnp.bfloat16)
    grad_w_out = (jnp.dot(hidden_act.T, grad_out, preferred_element_type=jnp.float32) * factor).astype(jnp.bfloat16)
    return (output, grad_in, grad_w_in, grad_w_out)
```

```python
import math

import jax
import jax.numpy as jnp
from jax import lax
from jax.experimental import pallas as pl
from jax.experimental.pallas import tpu as pltpu
from jax.sharding import PartitionSpec as P

root_two_pi = math.sqrt(2.0 / math.pi)
BF = jnp.bfloat16
F32 = jnp.float32
NT = (((1,), (1,)), ((), ()))
TN = (((0,), (0,)), ((), ()))
CHUNKS = (0, 1, 3, 2)
AWAY = (1, 3, 2)
TILE = 256


def gelu_pair(pre, grad):
    inner = root_two_pi * (pre + 0.044715 * pre * pre * pre)
    bent = jnp.tanh(inner)
    act = 0.5 * pre * (1.0 + bent)
    slope = 0.5 * (1.0 + bent) + 0.5 * pre * (1.0 - bent * bent) * root_two_pi * (
        1.0 + 3.0 * 0.044715 * pre * pre
    )
    return act, grad * slope


def kernel(
    tokens, grad_out, weight_in, weight_out,
    output, grad_in, grad_w_in, grad_w_out,
    panel, w_in, w_out, part, y_recv, z_send, z_own, z_recv, hidden,
    o_part, o_recv, x_send, x_recv, e_send, e_recv, final, gw_in, gw_out,
    load_sem, store_sem, gi_sem, go_sem,
    ag_recv, agz_send, agx_send, sib_recv, sib_send,
    y_rs, y_ss, z_rs, z_ss, p_rs, p_ss, hy_rs, hy_ss,
    o_rs, o_ss, x_rs, x_ss, e_rs, e_ss,
):
    row, col = lax.axis_index("row"), lax.axis_index("col")
    y, low = lax.rem(row, 4), lax.div(row, 4)
    core, x, z = lax.rem(col, 2), lax.rem(lax.div(col, 2), 4), lax.div(col, 8)

    def around(place, step):
        return lax.rem(place + step, 4)

    sibling = (row, z * 8 + x * 2 + (1 - core))
    partner = ((1 - low) * 4 + y, col)
    x_peer = {d: (row, z * 8 + around(x, d) * 2 + core) for d in AWAY}
    z_peer = {d: (row, around(z, d) * 8 + x * 2 + core) for d in AWAY}
    y_peer = {d: (low * 4 + around(y, d), col) for d in AWAY}
    sends = []

    def send(src, dst, send_sem, recv_sem, device):
        copy = pltpu.make_async_remote_copy(
            src_ref=src, dst_ref=dst, send_sem=send_sem, recv_sem=recv_sem,
            device_id=device, device_id_type=pl.DeviceIdType.MESH,
        )
        copy.start()
        sends.append(copy)

    def arrived(dst, send_sem, recv_sem, device):
        pltpu.make_async_remote_copy(
            src_ref=dst, dst_ref=dst, send_sem=send_sem, recv_sem=recv_sem,
            device_id=device, device_id_type=pl.DeviceIdType.MESH,
        ).wait_recv()

    own = panel.at[x, z, core]
    loads = [
        pltpu.make_async_copy(tokens, panel.at[x, z, core, 0], load_sem.at[0]),
        pltpu.make_async_copy(grad_out, panel.at[x, z, core, 1], load_sem.at[1]),
        pltpu.make_async_copy(weight_in, w_in, load_sem.at[2]),
        pltpu.make_async_copy(weight_out, w_out, load_sem.at[3]),
    ]
    for load in loads:
        load.start()
    peers = [sibling, partner] + [p[d] for p in (x_peer, z_peer, y_peer) for d in AWAY]
    barrier = pltpu.get_barrier_semaphore()
    for peer in peers:
        pl.semaphore_signal(barrier, inc=1, device_id=peer, device_id_type=pl.DeviceIdType.MESH)
    pl.semaphore_wait(barrier, len(peers))
    loads[0].wait()
    loads[1].wait()

    def to_sibling(dx, dz):
        block = panel.at[around(x, dx), around(z, dz), core]
        send(block, block, sib_send.at[dx, dz], sib_recv.at[dx, dz], sibling)

    def along_x(dz):
        block = panel.at[x, around(z, dz), core]
        for d in AWAY:
            send(block, block, agx_send.at[d, dz], ag_recv.at[4 - d, dz], x_peer[d])

    def gather_start():
        for d in AWAY:
            send(own, own, agz_send.at[d], ag_recv.at[0, 4 - d], z_peer[d])
        to_sibling(0, 0)
        along_x(0)

    def gather(dx, dz):
        block = panel.at[around(x, dx), around(z, dz), core]
        arrived(block, sib_send.at[dx, dz], ag_recv.at[dx, dz], sibling)
        to_sibling(dx, dz)
        if dx == 0:
            along_x(dz)

    def first(i):
        dx = CHUNKS[i]
        xk = around(x, dx)
        for dz in range(4):
            block = panel.at[xk, around(z, dz), 1 - core]
            arrived(block, sib_send.at[dx, dz], sib_recv.at[dx, dz], sibling)

        @pl.loop(0, 768 // TILE)
        def _(n):
            cols = pl.ds(pl.multiple_of(n * TILE, TILE), TILE)
            left = panel[xk, :, :, 0].reshape(128, 1536)
            pre = jnp.dot(left, w_in[:, cols], preferred_element_type=F32)
            part[i, :, :, 0, :, cols] = pre.astype(BF).reshape(4, 2, 16, TILE)
            left = panel[xk, :, :, 1].reshape(128, 1536)
            grad = lax.dot_general(left, w_out[cols, :], NT, preferred_element_type=F32)
            part[i, :, :, 1, :, cols] = grad.astype(BF).reshape(4, 2, 16, TILE)

        for d in AWAY:
            send(
                part.at[i, around(y, d)], y_recv.at[i, 3 - d],
                y_ss.at[i, d - 1], y_rs.at[i, 3 - d], y_peer[d],
            )

    def sum_y(i):
        for d in AWAY:
            arrived(y_recv.at[i, d - 1], y_ss.at[i, d - 1], y_rs.at[i, d - 1], sibling)

        def total(which):
            t = part[i, y, which].astype(F32)
            for j in range(3):
                t = t + y_recv[i, j, which].astype(F32)
            return t

        z_send[i] = total(1 - low).astype(BF)
        send(z_send.at[i], z_recv.at[i], z_ss.at[i], z_rs.at[i], partner)
        z_own[i] = total(low)

    def bend(i):
        xk = around(x, CHUNKS[i])
        arrived(z_recv.at[i], z_ss.at[i], z_rs.at[i], partner)
        total = z_own[i] + z_recv[i].astype(F32)
        act, pre_grad = gelu_pair(total[0], total[1])
        hidden[xk, y, low, 0] = act.astype(BF)
        hidden[xk, y, low, 1] = pre_grad.astype(BF)
        block = hidden.at[xk, y, low]
        send(block, block, p_ss.at[i], p_rs.at[i], partner)
        for d in AWAY:
            send(block, block, hy_ss.at[i, 0, d - 1], hy_rs.at[i, 0, 3 - d], y_peer[d])

    def pass_on(i):
        block = hidden.at[around(x, CHUNKS[i]), y, 1 - low]
        arrived(block, p_ss.at[i], p_rs.at[i], partner)
        for d in AWAY:
            send(block, block, hy_ss.at[i, 1, d - 1], hy_rs.at[i, 1, 3 - d], y_peer[d])

    def second(i):
        xk = around(x, CHUNKS[i])
        for d in AWAY:
            for k, half in ((0, low), (1, 1 - low)):
                block = hidden.at[xk, around(y, d), half]
                arrived(block, hy_ss.at[i, k, d - 1], hy_rs.at[i, k, d - 1], partner)

        @pl.loop(0, 1536 // TILE)
        def _(n):
            cols = pl.ds(pl.multiple_of(n * TILE, TILE), TILE)
            left = hidden[xk, :, :, 0].reshape(128, 768)
            out = jnp.dot(left, w_out[:, cols], preferred_element_type=F32)
            out = out.astype(BF).reshape(4, 2, 16, TILE)
            left = hidden[xk, :, :, 1].reshape(128, 768)
            back = lax.dot_general(left, w_in[cols, :], NT, preferred_element_type=F32)
            back = back.astype(BF).reshape(4, 2, 16, TILE)
            for c in range(2):
                o_part[i, c, :, 0, :, cols] = out[:, c]
                o_part[i, c, :, 1, :, cols] = back[:, c]

        send(o_part.at[i, 1 - core], o_recv.at[i], o_ss.at[i], o_rs.at[i], sibling)

    def sum_core(i):
        arrived(o_recv.at[i], o_ss.at[i], o_rs.at[i], sibling)

        @pl.loop(0, 4)
        def _(k):
            total = o_part[i, core, k].astype(F32) + o_recv[i, k].astype(F32)
            x_send[i, k] = total.astype(BF)

        if i > 0:
            d = CHUNKS[i]
            send(x_send.at[i], x_recv.at[3 - d], x_ss.at[d - 1], x_rs.at[3 - d], x_peer[d])

    def sum_x():
        for d in AWAY:
            arrived(x_recv.at[d - 1], x_ss.at[d - 1], x_rs.at[d - 1], sibling)
        for dz in AWAY + (0,):
            zk = around(z, dz)
            total = x_send[0, zk].astype(F32)
            for j in range(3):
                total = total + x_recv[j, zk].astype(F32)
            e_send[dz] = total.astype(BF)
            if dz > 0:
                send(
                    e_send.at[dz], e_recv.at[3 - dz], e_ss.at[dz - 1], e_rs.at[3 - dz], z_peer[dz]
                )

    def sum_z():
        for d in AWAY:
            arrived(e_recv.at[d - 1], e_ss.at[d - 1], e_rs.at[d - 1], sibling)
        total = e_send[0].astype(F32)
        for j in range(3):
            total = total + e_recv[j].astype(F32)
        final[...] = total.astype(BF)

    factor = 1.0 / math.sqrt(512)

    def gw_in_store(m):
        rows = pl.ds(pl.multiple_of(m * TILE, TILE), TILE)
        return pltpu.make_async_copy(gw_in.at[rows], grad_w_in.at[rows], gi_sem.at[m])

    def gw_out_store(m):
        rows = pl.ds(pl.multiple_of(m * TILE, TILE), TILE)
        return pltpu.make_async_copy(gw_out.at[rows], grad_w_out.at[rows], go_sem.at[m])

    def weight_in_grad(low_m, high_m):
        @pl.loop(low_m, high_m)
        def _(m):
            cols = pl.ds(pl.multiple_of(m * TILE, TILE), TILE)
            left = panel[:, :, :, 0, :, cols].reshape(512, TILE)
            right = hidden[:, :, :, 1].reshape(512, 768)
            grad = lax.dot_general(left, right, TN, preferred_element_type=F32)
            gw_in[cols, :] = (grad * factor).astype(BF)
            gw_in_store(m).start()

    def weight_out_grad(low_m, high_m):
        @pl.loop(low_m, high_m)
        def _(m):
            cols = pl.ds(pl.multiple_of(m * TILE, TILE), TILE)
            left = hidden[:, :, :, 0, :, cols].reshape(512, TILE)
            right = panel[:, :, :, 1].reshape(512, 1536)
            grad = lax.dot_general(left, right, TN, preferred_element_type=F32)
            gw_out[cols, :] = (grad * factor).astype(BF)
            gw_out_store(m).start()

    gather_start()
    for dz in AWAY:
        gather(0, dz)
    loads[2].wait()
    loads[3].wait()
    first(0)
    for dz in (0,) + AWAY:
        gather(1, dz)
        gather(3, dz)
    first(1)
    sum_y(0)
    first(2)
    for dz in (0,) + AWAY:
        gather(2, dz)
    bend(0)
    sum_y(1)
    first(3)
    pass_on(0)
    bend(1)
    sum_y(2)
    second(0)
    pass_on(1)
    bend(2)
    sum_y(3)
    sum_core(0)
    second(1)
    pass_on(2)
    bend(3)
    sum_core(1)
    second(2)
    pass_on(3)
    sum_core(2)
    second(3)
    weight_in_grad(0, 2)
    sum_core(3)
    weight_in_grad(2, 6)
    weight_out_grad(0, 2)
    sum_x()
    weight_out_grad(2, 3)
    sum_z()
    stores = [
        pltpu.make_async_copy(final.at[0], output, store_sem.at[0]),
        pltpu.make_async_copy(final.at[1], grad_in, store_sem.at[1]),
    ]
    for store in stores:
        store.start()
    for m in range(6):
        gw_in_store(m).wait()
    for m in range(3):
        gw_out_store(m).wait()
    for store in stores:
        store.wait()
    for copy in sends:
        copy.wait_send()


def shards(tokens, grad_out, weight_in, weight_out):
    dma = pltpu.SemaphoreType.DMA
    vmem = pltpu.VMEM
    like = jax.ShapeDtypeStruct
    return pl.pallas_call(
        kernel,
        out_shape=(
            like(tokens.shape, BF),
            like(tokens.shape, BF),
            like(weight_in.shape, BF),
            like(weight_out.shape, BF),
        ),
        in_specs=[pl.BlockSpec(memory_space=pl.ANY)] * 4,
        out_specs=[pl.BlockSpec(memory_space=pl.ANY)] * 4,
        scratch_shapes=[
            vmem((4, 4, 2, 2, 16, 1536), BF),
            vmem((1536, 768), BF),
            vmem((768, 1536), BF),
            vmem((4, 4, 2, 2, 16, 768), BF),
            vmem((4, 3, 2, 2, 16, 768), BF),
            vmem((4, 2, 16, 768), BF),
            vmem((4, 2, 16, 768), F32),
            vmem((4, 2, 16, 768), BF),
            vmem((4, 4, 2, 2, 16, 768), BF),
            vmem((4, 2, 4, 2, 16, 1536), BF),
            vmem((4, 4, 2, 16, 1536), BF),
            vmem((4, 4, 2, 16, 1536), BF),
            vmem((3, 4, 2, 16, 1536), BF),
            vmem((4, 2, 16, 1536), BF),
            vmem((3, 2, 16, 1536), BF),
            vmem((2, 16, 1536), BF),
            vmem((1536, 768), BF),
            vmem((768, 1536), BF),
            dma((4,)), dma((2,)), dma((6,)), dma((3,)),
            dma((4, 4)), dma((4,)), dma((4, 4)), dma((4, 4)), dma((4, 4)),
            dma((4, 3)), dma((4, 3)), dma((4,)), dma((4,)), dma((4,)), dma((4,)),
            dma((4, 2, 3)), dma((4, 2, 3)),
            dma((4,)), dma((4,)), dma((3,)), dma((3,)), dma((3,)), dma((3,)),
        ],
        compiler_params=pltpu.CompilerParams(
            collective_id=0, has_side_effects=True, vmem_limit_bytes=48 * 2**20
        ),
        name="block",
    )(tokens, grad_out, weight_in, weight_out)


def solution(mesh):
    placed = (P("col", "row"), P("col", "row"), P("row", "col"), P("col", "row"))
    return jax.shard_map(
        shards, mesh=mesh, in_specs=placed, out_specs=placed, check_vma=False
    )
```

```python
import math

import jax
import jax.numpy as jnp
from jax import lax
from jax.experimental import pallas as pl
from jax.experimental.pallas import tpu as pltpu
from jax.sharding import PartitionSpec as P

root_two_pi = math.sqrt(2.0 / math.pi)
BF = jnp.bfloat16
F32 = jnp.float32
NT = (((1,), (1,)), ((), ()))
TN = (((0,), (0,)), ((), ()))
AWAY = (1, 3, 2)
TILE = 256
CHUNKS = (0, 1, 3, 2)
STEPS = (
    ("A0", 0), ("A0", 1), ("A2", 0, 3, 0), ("A2", 0, 1, 0), ("A2", 0, 2, 0), ("A1", 0, 3),
    ("A1", 0, 1), ("A2", 1, 1, 0), ("A2", 1, 3, 0), ("c", 0, 0), ("A2", 1, 2, 0), ("A2", 0, 3, 3),
    ("A2", 0, 1, 3), ("A1", 0, 2), ("c", 0, 1), ("A1", 1, 1), ("A1", 1, 3), ("A2", 0, 2, 3),
    ("A2", 0, 3, 1), ("A2", 0, 1, 1), ("c", 2, 0), ("A2", 0, 2, 1), ("A2", 0, 1, 2),
    ("A2", 0, 3, 2), ("s", 0, 0), ("A1", 1, 2), ("c", 1, 0), ("A2", 0, 2, 2), ("A2", 1, 1, 1),
    ("A2", 1, 3, 1), ("s", 0, 1), ("b", 0, 0), ("c", 3, 0), ("A2", 1, 1, 3), ("A2", 1, 2, 1),
    ("A2", 1, 3, 3), ("s", 2, 0), ("b", 0, 1), ("p", 0, 0), ("A2", 1, 2, 3), ("c", 1, 1),
    ("A2", 1, 1, 2), ("A2", 1, 3, 2), ("s", 1, 0), ("b", 2, 0), ("c", 2, 1), ("A2", 1, 2, 2),
    ("p", 0, 1), ("s", 3, 0), ("b", 1, 0), ("c", 3, 1), ("p", 2, 0), ("g", 0, 0), ("b", 3, 0),
    ("p", 1, 0), ("s", 1, 1), ("h", 0, 0), ("p", 3, 0), ("s", 2, 1), ("b", 1, 1), ("g", 0, 1),
    ("p", 1, 1), ("b", 2, 1), ("X", 0, 0), ("s", 3, 1), ("h", 0, 1), ("p", 2, 1), ("g", 2, 0),
    ("b", 3, 1), ("g", 1, 0), ("X", 0, 1), ("h", 2, 0), ("p", 3, 1), ("g", 3, 0), ("h", 1, 0),
    ("WO", 0), ("g", 1, 1), ("h", 3, 0), ("X", 2, 0), ("WO", 1), ("g", 2, 1), ("X", 1, 0),
    ("h", 1, 1), ("g", 3, 1), ("h", 2, 1), ("X", 3, 0), ("WI", 0), ("WI", 1), ("h", 3, 1),
    ("WO", 2), ("X", 1, 1), ("WI", 2), ("WI", 3), ("WI", 4), ("X", 2, 1), ("WI", 5), ("Z", 0),
    ("X", 3, 1), ("Z", 1),
)


def gelu_pair(pre):
    inner = root_two_pi * (pre + 0.044715 * pre * pre * pre)
    bent = jnp.tanh(inner)
    act = 0.5 * pre * (1.0 + bent)
    slope = 0.5 * (1.0 + bent) + 0.5 * pre * (1.0 - bent * bent) * root_two_pi * (
        1.0 + 3.0 * 0.044715 * pre * pre
    )
    return act, slope


def kernel(
    tokens, grad_out, weight_in, weight_out,
    output, grad_in, grad_w_in, grad_w_out,
    panel, w_in, w_out, part, y_recv, z_send, z_own, z_recv, slope, hidden,
    o_part, o_recv, x_send, x_recv, e_send, e_recv, final, gw_in, gw_out,
    load_sem, store_sem, gi_sem, go_sem,
    az_rs, az_ss, ax_rs, ax_ss, sib_rs, sib_ss,
    y_rs, y_ss, z_rs, z_ss, p_rs, p_ss, hy_rs, hy_ss,
    o_rs, o_ss, x_rs, x_ss, e_rs, e_ss,
):
    row, col = lax.axis_index("row"), lax.axis_index("col")
    y, low = lax.rem(row, 4), lax.div(row, 4)
    core, x, z = lax.rem(col, 2), lax.rem(lax.div(col, 2), 4), lax.div(col, 8)

    def around(place, step):
        return lax.rem(place + step, 4)

    sibling = (row, z * 8 + x * 2 + (1 - core))
    partner = ((1 - low) * 4 + y, col)
    x_peer = {d: (row, z * 8 + around(x, d) * 2 + core) for d in AWAY}
    z_peer = {d: (row, around(z, d) * 8 + x * 2 + core) for d in AWAY}
    y_peer = {d: (low * 4 + around(y, d), col) for d in AWAY}
    sends = []

    def send(src, dst, send_sem, recv_sem, device):
        copy = pltpu.make_async_remote_copy(
            src_ref=src, dst_ref=dst, send_sem=send_sem, recv_sem=recv_sem,
            device_id=device, device_id_type=pl.DeviceIdType.MESH,
        )
        copy.start()
        sends.append(copy)

    def arrived(dst, send_sem, recv_sem):
        pltpu.make_async_remote_copy(
            src_ref=dst, dst_ref=dst, send_sem=send_sem, recv_sem=recv_sem,
            device_id=sibling, device_id_type=pl.DeviceIdType.MESH,
        ).wait_recv()

    loads = [
        pltpu.make_async_copy(tokens, panel.at[0, z, core, x], load_sem.at[0]),
        pltpu.make_async_copy(grad_out, panel.at[1, z, core, x], load_sem.at[1]),
        pltpu.make_async_copy(weight_in, w_in, load_sem.at[2]),
        pltpu.make_async_copy(weight_out, w_out, load_sem.at[3]),
    ]
    for load in loads:
        load.start()
    peers = [sibling, partner] + [p[d] for p in (x_peer, z_peer, y_peer) for d in AWAY]
    barrier = pltpu.get_barrier_semaphore()
    for peer in peers:
        pl.semaphore_signal(barrier, inc=1, device_id=peer, device_id_type=pl.DeviceIdType.MESH)
    pl.semaphore_wait(barrier, len(peers))

    def block(a, dx, dz, c):
        return panel.at[a, around(z, dz), c, around(x, dx)]

    def to_sibling(a, dx, dz):
        mine = block(a, dx, dz, core)
        send(mine, mine, sib_ss.at[a, dx, dz], sib_rs.at[a, dx, dz], sibling)

    def along_x(a, dz):
        mine = block(a, 0, dz, core)
        for d in AWAY:
            send(mine, mine, ax_ss.at[a, d, dz], ax_rs.at[a, 4 - d, dz], x_peer[d])

    def gather_own(a):
        loads[a].wait()
        along_x(a, 0)
        mine = block(a, 0, 0, core)
        for d in AWAY:
            send(mine, mine, az_ss.at[a, d], az_rs.at[a, 4 - d], z_peer[d])
        to_sibling(a, 0, 0)

    def gather_z(a, dz):
        arrived(block(a, 0, dz, core), az_ss.at[a, dz], az_rs.at[a, dz])
        along_x(a, dz)
        to_sibling(a, 0, dz)

    def gather_x(a, dx, dz):
        arrived(block(a, dx, dz, core), ax_ss.at[a, dx, dz], ax_rs.at[a, dx, dz])
        to_sibling(a, dx, dz)

    ready = set()

    def first(i, a):
        dz = CHUNKS[i]
        zk = around(z, dz)
        for dx in range(4):
            arrived(block(a, dx, dz, 1 - core), sib_ss.at[a, dx, dz], sib_rs.at[a, dx, dz])
        if a not in ready:
            ready.add(a)
            loads[2 + a].wait()

        @pl.loop(0, 768 // TILE)
        def _(n):
            cols = pl.ds(pl.multiple_of(n * TILE, TILE), TILE)
            left = panel[a, zk].reshape(128, 1536)
            if a == 0:
                total = jnp.dot(left, w_in[:, cols], preferred_element_type=F32)
            else:
                total = lax.dot_general(left, w_out[cols, :], NT, preferred_element_type=F32)
            part[i, a, :, :, :, cols] = total.astype(BF).reshape(4, 2, 16, TILE)

        for d in AWAY:
            send(
                part.at[i, a, around(y, d)], y_recv.at[i, a, 3 - d],
                y_ss.at[i, a, d - 1], y_rs.at[i, a, 3 - d], y_peer[d],
            )

    def sum_y(i, a):
        for d in AWAY:
            arrived(y_recv.at[i, a, d - 1], y_ss.at[i, a, d - 1], y_rs.at[i, a, d - 1])

        def total(which):
            t = part[i, a, y, which].astype(F32)
            for j in range(3):
                t = t + y_recv[i, a, j, which].astype(F32)
            return t

        z_send[i, a] = total(1 - low).astype(BF)
        send(z_send.at[i, a], z_recv.at[i, a], z_ss.at[i, a], z_rs.at[i, a], partner)
        z_own[i, a] = total(low)

    def bend(i, a):
        zk = around(z, CHUNKS[i])
        arrived(z_recv.at[i, a], z_ss.at[i, a], z_rs.at[i, a])
        total = z_own[i, a] + z_recv[i, a].astype(F32)
        if a == 0:
            act, bent = gelu_pair(total)
            slope[i] = bent
            hidden[a, zk, y, low] = act.astype(BF)
        else:
            hidden[a, zk, y, low] = (total * slope[i]).astype(BF)
        mine = hidden.at[a, zk, y, low]
        send(mine, mine, p_ss.at[i, a], p_rs.at[i, a], partner)

    def pass_on(i, a):
        zk = around(z, CHUNKS[i])
        arrived(hidden.at[a, zk, y, 1 - low], p_ss.at[i, a], p_rs.at[i, a])
        both = hidden.at[a, zk, y]
        for d in AWAY:
            send(both, both, hy_ss.at[i, a, d - 1], hy_rs.at[i, a, 3 - d], y_peer[d])

    def second(i, a):
        zk = around(z, CHUNKS[i])
        for d in AWAY:
            both = hidden.at[a, zk, around(y, d)]
            arrived(both, hy_ss.at[i, a, d - 1], hy_rs.at[i, a, d - 1])

        @pl.loop(0, 1536 // TILE)
        def _(n):
            cols = pl.ds(pl.multiple_of(n * TILE, TILE), TILE)
            left = hidden[a, zk].reshape(128, 768)
            if a == 0:
                total = jnp.dot(left, w_out[:, cols], preferred_element_type=F32)
            else:
                total = lax.dot_general(left, w_in[cols, :], NT, preferred_element_type=F32)
            o_part[i, a, :, :, :, cols] = total.astype(BF).reshape(2, 4, 16, TILE)

        send(
            o_part.at[i, a, 1 - core], o_recv.at[i, a], o_ss.at[i, a], o_rs.at[i, a], sibling
        )

    def sum_core(i, a):
        arrived(o_recv.at[i, a], o_ss.at[i, a], o_rs.at[i, a])
        for d in (2, 1, 3, 0):
            xk = around(x, d)
            total = o_part[i, a, core, xk].astype(F32) + o_recv[i, a, xk].astype(F32)
            x_send[i, a, d] = total.astype(BF)
            if d > 0:
                send(
                    x_send.at[i, a, d], x_recv.at[i, a, 3 - d],
                    x_ss.at[i, a, d - 1], x_rs.at[i, a, 3 - d], x_peer[d],
                )

    def sum_x(i, a):
        for d in AWAY:
            arrived(x_recv.at[i, a, d - 1], x_ss.at[i, a, d - 1], x_rs.at[i, a, d - 1])
        total = x_send[i, a, 0].astype(F32)
        for j in range(3):
            total = total + x_recv[i, a, j].astype(F32)
        e_send[i, a] = total.astype(BF)
        dz = CHUNKS[i]
        if dz > 0:
            send(
                e_send.at[i, a], e_recv.at[a, 3 - dz],
                e_ss.at[a, dz - 1], e_rs.at[a, 3 - dz], z_peer[dz],
            )

    stores = []

    def sum_z(a):
        for d in AWAY:
            arrived(e_recv.at[a, d - 1], e_ss.at[a, d - 1], e_rs.at[a, d - 1])
        total = e_send[CHUNKS.index(0), a].astype(F32)
        for j in range(3):
            total = total + e_recv[a, j].astype(F32)
        final[a] = total.astype(BF)
        store = pltpu.make_async_copy(final.at[a], (output, grad_in)[a], store_sem.at[a])
        store.start()
        stores.append(store)

    factor = 1.0 / math.sqrt(512)

    def weight_in_grad(m):
        cols = pl.ds(m * TILE, TILE)
        left = panel[0, :, :, :, :, cols].reshape(512, TILE)
        grad = lax.dot_general(left, hidden[1].reshape(512, 768), TN, preferred_element_type=F32)
        gw_in[cols, :] = (grad * factor).astype(BF)
        store = pltpu.make_async_copy(gw_in.at[cols], grad_w_in.at[cols], gi_sem.at[m])
        store.start()
        stores.append(store)

    def weight_out_grad(m):
        cols = pl.ds(m * TILE, TILE)
        left = hidden[0, :, :, :, :, cols].reshape(512, TILE)
        grad = lax.dot_general(left, panel[1].reshape(512, 1536), TN, preferred_element_type=F32)
        gw_out[cols, :] = (grad * factor).astype(BF)
        store = pltpu.make_async_copy(gw_out.at[cols], grad_w_out.at[cols], go_sem.at[m])
        store.start()
        stores.append(store)

    does = {
        "A0": gather_own, "A1": gather_z, "A2": gather_x, "c": first, "s": sum_y, "b": bend,
        "p": pass_on, "g": second, "h": sum_core, "X": sum_x, "Z": sum_z,
        "WI": weight_in_grad, "WO": weight_out_grad,
    }
    for name, *where in STEPS:
        does[name](*where)
    for store in stores:
        store.wait()
    for copy in sends:
        copy.wait_send()


def shards(tokens, grad_out, weight_in, weight_out):
    dma = pltpu.SemaphoreType.DMA
    vmem = pltpu.VMEM
    like = jax.ShapeDtypeStruct
    return pl.pallas_call(
        kernel,
        out_shape=(
            like(tokens.shape, BF),
            like(tokens.shape, BF),
            like(weight_in.shape, BF),
            like(weight_out.shape, BF),
        ),
        in_specs=[pl.BlockSpec(memory_space=pl.ANY)] * 4,
        out_specs=[pl.BlockSpec(memory_space=pl.ANY)] * 4,
        scratch_shapes=[
            vmem((2, 4, 2, 4, 16, 1536), BF),
            vmem((1536, 768), BF),
            vmem((768, 1536), BF),
            vmem((4, 2, 4, 2, 16, 768), BF),
            vmem((4, 2, 3, 2, 16, 768), BF),
            vmem((4, 2, 16, 768), BF),
            vmem((4, 2, 16, 768), F32),
            vmem((4, 2, 16, 768), BF),
            vmem((4, 16, 768), F32),
            vmem((2, 4, 4, 2, 16, 768), BF),
            vmem((4, 2, 2, 4, 16, 1536), BF),
            vmem((4, 2, 4, 16, 1536), BF),
            vmem((4, 2, 4, 16, 1536), BF),
            vmem((4, 2, 3, 16, 1536), BF),
            vmem((4, 2, 16, 1536), BF),
            vmem((2, 3, 16, 1536), BF),
            vmem((2, 16, 1536), BF),
            vmem((1536, 768), BF),
            vmem((768, 1536), BF),
            dma((4,)), dma((2,)), dma((6,)), dma((3,)),
            dma((2, 4)), dma((2, 4)), dma((2, 4, 4)), dma((2, 4, 4)), dma((2, 4, 4)), dma((2, 4, 4)),
            dma((4, 2, 3)), dma((4, 2, 3)), dma((4, 2)), dma((4, 2)), dma((4, 2)), dma((4, 2)),
            dma((4, 2, 3)), dma((4, 2, 3)),
            dma((4, 2)), dma((4, 2)), dma((4, 2, 3)), dma((4, 2, 3)), dma((2, 3)), dma((2, 3)),
        ],
        compiler_params=pltpu.CompilerParams(
            collective_id=0, has_side_effects=True, vmem_limit_bytes=VMEM_LIMIT
        ),
        name="block",
    )(tokens, grad_out, weight_in, weight_out)


VMEM_LIMIT = 60 * 2**20


def solution(mesh):
    placed = (P("col", "row"), P("col", "row"), P("row", "col"), P("col", "row"))
    return jax.shard_map(
        shards, mesh=mesh, in_specs=placed, out_specs=placed, check_vma=False
    )
```

```python
import math

import jax
import jax.numpy as jnp
from jax import lax
from jax.experimental import pallas as pl
from jax.experimental.pallas import tpu as pltpu
from jax.sharding import PartitionSpec as P

root_two_pi = math.sqrt(2.0 / math.pi)
BF = jnp.bfloat16
F32 = jnp.float32
NT = (((1,), (1,)), ((), ()))
TN = (((0,), (0,)), ((), ()))
AWAY = (1, 3, 2)
TILE = 256
CHUNKS = (0, 3, 1, 2)
RELAY_X = ((1, 1), (1, 3))
RELAY_Z = ()
RELAY_Y_SUM = ((1, 1), (2, 1), (3, 0), (3, 1))
RELAY_Y = ((0, 0), (0, 1), (1, 0), (2, 0), (3, 0))
RELAY_X_SUM = ()
ON, BACK = (1, 3), (3, 1)
STEPS = (
    ("A0", 0), ("A0", 1), ("A2", 0, 3, 0), ("A2", 0, 1, 0), ("A2", 0, 2, 0), ("A1", 0, 3),
    ("A1", 0, 1), ("A2", 1, 1, 0), ("A2", 1, 3, 0), ("c", 0, 0), ("A2", 1, 2, 0), ("A2", 0, 3, 3),
    ("A2", 0, 1, 3), ("A1", 0, 2), ("c", 0, 1), ("A1", 1, 1), ("A1", 1, 3), ("A2", 0, 2, 3),
    ("A2", 0, 3, 1), ("A2", 0, 1, 1), ("c", 1, 0), ("A2", 0, 2, 1), ("A2", 0, 3, 2),
    ("A2", 0, 1, 2), ("s", 0, 0), ("A1", 1, 2), ("c", 2, 0), ("A2", 0, 2, 2), ("A2", 1, 1, 1),
    ("A2", 1, 3, 1), ("s", 0, 1), ("A2", 1, 3, 3), ("A2", 1, 1, 3), ("b", 0, 0), ("c", 3, 0),
    ("s", 1, 0), ("A2", 1, 1, 2), ("A2", 1, 3, 2), ("b", 0, 1), ("A2", 1, 2, 2), ("A2", 1, 2, 1),
    ("s", 2, 0), ("f", 0, 0), ("c", 3, 1), ("r", 3, 0), ("A2", 1, 2, 3), ("b", 1, 0), ("c", 2, 1),
    ("f", 0, 1), ("c", 1, 1), ("g", 0, 0), ("r", 3, 1), ("b", 2, 0), ("s", 3, 0), ("r", 2, 1),
    ("h", 0, 0), ("f", 1, 0), ("g", 0, 1), ("r", 1, 1), ("b", 3, 0), ("s", 3, 1), ("f", 2, 0),
    ("h", 0, 1), ("g", 1, 0), ("s", 2, 1), ("f", 3, 0), ("X", 0, 0), ("s", 1, 1), ("b", 3, 1),
    ("g", 2, 0), ("h", 1, 0), ("b", 2, 1), ("g", 3, 0), ("b", 1, 1), ("h", 2, 0), ("WO", 0),
    ("h", 3, 0), ("g", 3, 1), ("WO", 1), ("g", 2, 1), ("h", 3, 1), ("X", 2, 0), ("g", 1, 1),
    ("h", 2, 1), ("X", 3, 0), ("WO", 2), ("X", 1, 0), ("h", 1, 1), ("WI", 0), ("X", 3, 1),
    ("WI", 1), ("WI", 2), ("WI", 3), ("X", 2, 1), ("WI", 4), ("WI", 5), ("X", 1, 1), ("X", 0, 1),
    ("Z", 0), ("Z", 1),
)


def gelu_pair(pre):
    inner = root_two_pi * (pre + 0.044715 * pre * pre * pre)
    bent = jnp.tanh(inner)
    act = 0.5 * pre * (1.0 + bent)
    slope = 0.5 * (1.0 + bent) + 0.5 * pre * (1.0 - bent * bent) * root_two_pi * (
        1.0 + 3.0 * 0.044715 * pre * pre
    )
    return act, slope


def kernel(
    tokens, grad_out, weight_in, weight_out,
    output, grad_in, grad_w_in, grad_w_out,
    panel, w_in, w_out, part, y_join, y_recv, z_send, z_recv, slope, hidden,
    o_part, o_recv, x_send, x_join, x_recv, e_send, e_recv, load_sem,
    az_rs, az_ss, ax_rs, ax_ss, sib_rs, sib_ss,
    y_rs, y_ss, z_rs, z_ss, hy_rs, hy_ss,
    o_rs, o_ss, x_rs, x_ss, e_rs, e_ss,
):
    row, col = lax.axis_index("row"), lax.axis_index("col")
    y, low = lax.rem(row, 4), lax.div(row, 4)
    core, x, z = lax.rem(col, 2), lax.rem(lax.div(col, 2), 4), lax.div(col, 8)

    def around(place, step):
        return lax.rem(place + step, 4)

    sibling = (row, z * 8 + x * 2 + (1 - core))
    partner = ((1 - low) * 4 + y, col)
    x_peer = {d: (row, z * 8 + around(x, d) * 2 + core) for d in AWAY}
    z_peer = {d: (row, around(z, d) * 8 + x * 2 + core) for d in AWAY}
    y_peer = {d: (low * 4 + around(y, d), col) for d in AWAY}
    sends = []

    def send(src, dst, send_sem, recv_sem, device):
        copy = pltpu.make_async_remote_copy(
            src_ref=src, dst_ref=dst, send_sem=send_sem, recv_sem=recv_sem,
            device_id=device, device_id_type=pl.DeviceIdType.MESH,
        )
        copy.start()
        sends.append(copy)

    def arrived(dst, send_sem, recv_sem):
        pltpu.make_async_remote_copy(
            src_ref=dst, dst_ref=dst, send_sem=send_sem, recv_sem=recv_sem,
            device_id=sibling, device_id_type=pl.DeviceIdType.MESH,
        ).wait_recv()

    loads = [
        pltpu.make_async_copy(tokens, panel.at[0, z, core, x], load_sem.at[0]),
        pltpu.make_async_copy(grad_out, panel.at[1, z, core, x], load_sem.at[1]),
        pltpu.make_async_copy(weight_in, w_in, load_sem.at[2]),
        pltpu.make_async_copy(weight_out, w_out, load_sem.at[3]),
    ]
    for load in loads:
        load.start()
    peers = [sibling, partner] + [p[d] for p in (x_peer, z_peer, y_peer) for d in AWAY]
    barrier = pltpu.get_barrier_semaphore()
    for peer in peers:
        pl.semaphore_signal(barrier, inc=1, device_id=peer, device_id_type=pl.DeviceIdType.MESH)
    pl.semaphore_wait(barrier, len(peers))

    def block(a, dx, dz, c):
        return panel.at[a, around(z, dz), c, around(x, dx)]

    def to_sibling(a, dx, dz):
        mine = block(a, dx, dz, core)
        send(mine, mine, sib_ss.at[a, dx, dz], sib_rs.at[a, dx, dz], sibling)

    def along_x(a, dz):
        mine = block(a, 0, dz, core)
        for d in AWAY[:2] if (a, dz) in RELAY_X else AWAY:
            send(mine, mine, ax_ss.at[a, d, dz], ax_rs.at[a, 4 - d, dz], x_peer[d])

    def gather_own(a):
        loads[a].wait()
        along_x(a, 0)
        mine = block(a, 0, 0, core)
        for d in AWAY[:2] if a in RELAY_Z else AWAY:
            send(mine, mine, az_ss.at[a, d], az_rs.at[a, 4 - d], z_peer[d])
        to_sibling(a, 0, 0)

    def gather_z(a, dz):
        arrived(block(a, 0, dz, core), az_ss.at[a, dz], az_rs.at[a, dz])
        along_x(a, dz)
        if a in RELAY_Z and dz == BACK[a]:
            mine = block(a, 0, dz, core)
            send(mine, mine, az_ss.at[a, 2], az_rs.at[a, 2], z_peer[ON[a]])
        to_sibling(a, 0, dz)

    def gather_x(a, dx, dz):
        arrived(block(a, dx, dz, core), ax_ss.at[a, dx, dz], ax_rs.at[a, dx, dz])
        if (a, dz) in RELAY_X and dx == BACK[a]:
            mine = block(a, dx, dz, core)
            send(mine, mine, ax_ss.at[a, 2, dz], ax_rs.at[a, 2, dz], x_peer[ON[a]])
        to_sibling(a, dx, dz)

    ready = set()

    def first(i, a):
        dz = CHUNKS[i]
        zk = around(z, dz)
        for dx in range(4):
            arrived(block(a, dx, dz, 1 - core), sib_ss.at[a, dx, dz], sib_rs.at[a, dx, dz])
        if a not in ready:
            ready.add(a)
            loads[2 + a].wait()

        @pl.loop(0, 768 // TILE)
        def _(n):
            cols = pl.ds(pl.multiple_of(n * TILE, TILE), TILE)
            left = panel[a, zk].reshape(128, 1536)
            if a == 0:
                total = jnp.dot(left, w_in[:, cols], preferred_element_type=F32)
            else:
                total = lax.dot_general(left, w_out[cols, :], NT, preferred_element_type=F32)
            part[i, a, :, :, :, cols] = total.astype(BF).reshape(4, 2, 16, TILE)

        def to_y(d, slot, device):
            send(
                part.at[i, a, around(y, d)], y_recv.at[i, a, slot],
                y_ss.at[i, a, slot], y_rs.at[i, a, slot], y_peer[device],
            )

        if (i, a) in RELAY_Y_SUM:
            to_y(2, 0, ON[a])
            to_y(BACK[a], 1, BACK[a])
        else:
            for d in AWAY:
                to_y(d, 3 - d, d)

    def y_arrived(i, a, slot):
        arrived(y_recv.at[i, a, slot], y_ss.at[i, a, slot], y_rs.at[i, a, slot])

    def join_y(i, a):
        y_arrived(i, a, 0)
        total = part[i, a, around(y, ON[a])].astype(F32) + y_recv[i, a, 0].astype(F32)
        y_join[i, a] = total.astype(BF)
        send(
            y_join.at[i, a], y_recv.at[i, a, 2],
            y_ss.at[i, a, 2], y_rs.at[i, a, 2], y_peer[ON[a]],
        )

    def sum_y(i, a):
        slots = (1, 2) if (i, a) in RELAY_Y_SUM else (0, 1, 2)
        total = part[i, a, y].astype(F32)
        for slot in slots:
            y_arrived(i, a, slot)
        for slot in slots:
            total = total + y_recv[i, a, slot].astype(F32)
        z_send[i, a] = total.astype(BF)
        send(z_send.at[i, a], z_recv.at[i, a], z_ss.at[i, a], z_rs.at[i, a], partner)

    def bend(i, a):
        zk = around(z, CHUNKS[i])
        arrived(z_recv.at[i, a], z_ss.at[i, a], z_rs.at[i, a])
        total = z_send[i, a].astype(F32) + z_recv[i, a].astype(F32)
        if a == 0:
            act, bent = gelu_pair(total)
            slope[i] = bent
            hidden[a, zk, y] = act.astype(BF)
        else:
            hidden[a, zk, y] = (total * slope[i]).astype(BF)
        both = hidden.at[a, zk, y]
        for d in AWAY[:2] if (i, a) in RELAY_Y else AWAY:
            send(both, both, hy_ss.at[i, a, d - 1], hy_rs.at[i, a, 3 - d], y_peer[d])

    def hidden_arrived(i, a, d):
        both = hidden.at[a, around(z, CHUNKS[i]), around(y, d)]
        arrived(both, hy_ss.at[i, a, d - 1], hy_rs.at[i, a, d - 1])
        return both

    def pass_on(i, a):
        both = hidden_arrived(i, a, BACK[a])
        send(both, both, hy_ss.at[i, a, 1], hy_rs.at[i, a, 1], y_peer[ON[a]])

    def second(i, a):
        zk = around(z, CHUNKS[i])
        for d in (ON[a], 2) if (i, a) in RELAY_Y else AWAY:
            hidden_arrived(i, a, d)

        @pl.loop(0, 1536 // TILE)
        def _(n):
            cols = pl.ds(pl.multiple_of(n * TILE, TILE), TILE)
            left = hidden[a, zk].reshape(128, 768)
            if a == 0:
                total = jnp.dot(left, w_out[:, cols], preferred_element_type=F32)
            else:
                total = lax.dot_general(left, w_in[cols, :], NT, preferred_element_type=F32)
            o_part[i, a, :, :, :, cols] = total.astype(BF).reshape(2, 4, 16, TILE)

        send(
            o_part.at[i, a, 1 - core], o_recv.at[i, a], o_ss.at[i, a], o_rs.at[i, a], sibling
        )

    def to_x(i, a, src, slot, device):
        send(
            src, x_recv.at[i, a, slot], x_ss.at[i, a, slot], x_rs.at[i, a, slot], x_peer[device]
        )

    def x_arrived(i, a, slot):
        arrived(x_recv.at[i, a, slot], x_ss.at[i, a, slot], x_rs.at[i, a, slot])

    def sum_core(i, a):
        arrived(o_recv.at[i, a], o_ss.at[i, a], o_rs.at[i, a])
        relay = (i, a) in RELAY_X_SUM
        for d in (2, BACK[a], ON[a], 0):
            xk = around(x, d)
            total = o_part[i, a, core, xk].astype(F32) + o_recv[i, a, xk].astype(F32)
            x_send[i, a, d] = total.astype(BF)
            if relay and d == 2:
                to_x(i, a, x_send.at[i, a, d], 0, ON[a])
            elif relay and d == BACK[a]:
                to_x(i, a, x_send.at[i, a, d], 1, d)
            elif not relay and d > 0:
                to_x(i, a, x_send.at[i, a, d], 3 - d, d)

    def join_x(i, a):
        x_arrived(i, a, 0)
        total = x_send[i, a, ON[a]].astype(F32) + x_recv[i, a, 0].astype(F32)
        x_join[i, a] = total.astype(BF)
        to_x(i, a, x_join.at[i, a], 2, ON[a])

    def sum_x(i, a):
        slots = (1, 2) if (i, a) in RELAY_X_SUM else (0, 1, 2)
        for slot in slots:
            x_arrived(i, a, slot)
        total = x_send[i, a, 0].astype(F32)
        for slot in slots:
            total = total + x_recv[i, a, slot].astype(F32)
        e_send[i, a] = total.astype(BF)
        dz = CHUNKS[i]
        if dz > 0:
            send(
                e_send.at[i, a], e_recv.at[a, 3 - dz],
                e_ss.at[a, dz - 1], e_rs.at[a, 3 - dz], z_peer[dz],
            )

    def sum_z(a):
        for d in AWAY:
            arrived(e_recv.at[a, d - 1], e_ss.at[a, d - 1], e_rs.at[a, d - 1])
        total = e_send[CHUNKS.index(0), a].astype(F32)
        for j in range(3):
            total = total + e_recv[a, j].astype(F32)
        (output, grad_in)[a][...] = total.astype(BF)

    factor = 1.0 / math.sqrt(512)

    def weight_in_grad(m):
        cols = pl.ds(m * TILE, TILE)
        left = panel[0, :, :, :, :, cols].reshape(512, TILE)
        grad = lax.dot_general(left, hidden[1].reshape(512, 768), TN, preferred_element_type=F32)
        grad_w_in[cols, :] = (grad * factor).astype(BF)

    def weight_out_grad(m):
        cols = pl.ds(m * TILE, TILE)
        left = hidden[0, :, :, :, :, cols].reshape(512, TILE)
        grad = lax.dot_general(left, panel[1].reshape(512, 1536), TN, preferred_element_type=F32)
        grad_w_out[cols, :] = (grad * factor).astype(BF)

    does = {
        "A0": gather_own, "A1": gather_z, "A2": gather_x, "c": first, "s": sum_y, "b": bend,
        "r": join_y, "f": pass_on, "g": second, "h": sum_core, "q": join_x, "X": sum_x, "Z": sum_z,
        "WI": weight_in_grad, "WO": weight_out_grad,
    }
    for name, *where in STEPS:
        does[name](*where)
    for copy in sends:
        copy.wait_send()


def write_out(*refs):
    n = len(refs) // 2
    copies = [pltpu.make_async_copy(refs[j], refs[n + j], refs[-1].at[j]) for j in range(n)]
    for copy in copies:
        copy.start()
    for copy in copies:
        copy.wait()


def shards(tokens, grad_out, weight_in, weight_out):
    dma = pltpu.SemaphoreType.DMA
    vmem = pltpu.VMEM
    like = jax.ShapeDtypeStruct
    shapes = (
        like(tokens.shape, BF), like(tokens.shape, BF),
        like(weight_in.shape, BF), like(weight_out.shape, BF),
    )
    results = pl.pallas_call(
        kernel,
        out_shape=shapes,
        in_specs=[pl.BlockSpec(memory_space=IN_SPACE)] * 4,
        out_specs=[pl.BlockSpec(memory_space=OUT_SPACE)] * 4,
        scratch_shapes=[
            vmem((2, 4, 2, 4, 16, 1536), BF),
            vmem((1536, 768), BF),
            vmem((768, 1536), BF),
            vmem((4, 2, 4, 2, 16, 768), BF),
            vmem((4, 2, 2, 16, 768), BF),
            vmem((4, 2, 3, 2, 16, 768), BF),
            vmem((4, 2, 2, 16, 768), BF),
            vmem((4, 2, 2, 16, 768), BF),
            vmem((4, 2, 16, 768), F32),
            vmem((2, 4, 4, 2, 16, 768), BF),
            vmem((4, 2, 2, 4, 16, 1536), BF),
            vmem((4, 2, 4, 16, 1536), BF),
            vmem((4, 2, 4, 16, 1536), BF),
            vmem((4, 2, 16, 1536), BF),
            vmem((4, 2, 3, 16, 1536), BF),
            vmem((4, 2, 16, 1536), BF),
            vmem((2, 3, 16, 1536), BF),
            dma((4,)),
            dma((2, 4)), dma((2, 4)), dma((2, 4, 4)), dma((2, 4, 4)), dma((2, 4, 4)), dma((2, 4, 4)),
            dma((4, 2, 3)), dma((4, 2, 3)), dma((4, 2)), dma((4, 2)), dma((4, 2, 3)), dma((4, 2, 3)),
            dma((4, 2)), dma((4, 2)), dma((4, 2, 3)), dma((4, 2, 3)), dma((2, 3)), dma((2, 3)),
        ],
        compiler_params=pltpu.CompilerParams(
            collective_id=0, has_side_effects=True, vmem_limit_bytes=VMEM_LIMIT
        ),
        name="block",
    )(tokens, grad_out, weight_in, weight_out)
    return pl.pallas_call(
        write_out,
        out_shape=shapes,
        in_specs=[pl.BlockSpec(memory_space=MID_SPACE)] * 4,
        out_specs=[pl.BlockSpec(memory_space=pl.ANY)] * 4,
        scratch_shapes=[dma((4,))],
        compiler_params=pltpu.CompilerParams(vmem_limit_bytes=2**20),
        name="write_out",
    )(*results)


IN_SPACE = pltpu.HBM
OUT_SPACE = pltpu.VMEM
MID_SPACE = pltpu.VMEM
VMEM_LIMIT = 48 * 2**20


def solution(mesh):
    placed = (P("col", "row"), P("col", "row"), P("row", "col"), P("col", "row"))
    return jax.shard_map(
        shards, mesh=mesh, in_specs=placed, out_specs=placed, check_vma=False
    )
```

```python
import math

import jax
import jax.numpy as jnp
from jax import lax
from jax.experimental import pallas as pl
from jax.experimental.pallas import tpu as pltpu
from jax.sharding import PartitionSpec as P

root_two_pi = math.sqrt(2.0 / math.pi)
BF = jnp.bfloat16
F32 = jnp.float32
NT = (((1,), (1,)), ((), ()))
TN = (((0,), (0,)), ((), ()))
AWAY = (1, 3, 2)
TILE = 256
TILE_C = 768
TILE_G = 1536
CHUNKS = (0, 3, 1, 2)
RELAY_X = ((1, 1), (1, 3))
RELAY_Z = ()
RELAY_Y_SUM = ((1, 1), (2, 1), (3, 0), (3, 1))
RELAY_Y = ((0, 0), (0, 1), (1, 0), (2, 0), (3, 0))
RELAY_X_SUM = ()
ON, BACK = (1, 3), (3, 1)
STEPS = (
    ("A0", 0), ("A0", 1), ("A2", 0, 3, 0), ("A1", 0, 3), ("A2", 0, 2, 0), ("A1", 0, 1),
    ("A2", 0, 1, 0), ("A2", 1, 1, 0), ("A2", 1, 3, 0), ("c", 0, 0), ("A2", 1, 2, 0), ("A1", 0, 2),
    ("A2", 0, 3, 3), ("c", 0, 1), ("A2", 0, 1, 3), ("A1", 1, 1), ("A2", 0, 2, 3), ("A2", 0, 3, 1),
    ("A2", 0, 1, 1), ("c", 1, 0), ("A2", 0, 2, 1), ("A2", 0, 1, 2), ("A1", 1, 2), ("s", 0, 0),
    ("A2", 0, 3, 2), ("A1", 1, 3), ("c", 2, 0), ("A2", 0, 2, 2), ("A2", 1, 1, 1), ("c", 3, 0),
    ("b", 0, 0), ("s", 1, 0), ("A2", 1, 3, 2), ("A2", 1, 3, 3), ("A2", 1, 2, 2), ("A2", 1, 1, 3),
    ("A2", 1, 1, 2), ("A2", 1, 2, 1), ("A2", 1, 3, 1), ("r", 3, 0), ("c", 3, 1), ("s", 2, 0),
    ("c", 2, 1), ("A2", 1, 2, 3), ("b", 1, 0), ("s", 0, 1), ("c", 1, 1), ("s", 3, 0), ("r", 3, 1),
    ("r", 2, 1), ("b", 2, 0), ("f", 1, 0), ("r", 1, 1), ("b", 3, 0), ("b", 0, 1), ("s", 3, 1),
    ("s", 2, 1), ("f", 2, 0), ("g", 1, 0), ("f", 3, 0), ("s", 1, 1), ("b", 3, 1), ("h", 1, 0),
    ("g", 2, 0), ("b", 2, 1), ("g", 3, 0), ("h", 2, 0), ("b", 1, 1), ("g", 3, 1), ("h", 3, 0),
    ("f", 0, 1), ("f", 0, 0), ("g", 2, 1), ("h", 3, 1), ("X", 1, 0), ("X", 2, 0), ("g", 1, 1),
    ("h", 2, 1), ("g", 0, 1), ("g", 0, 0), ("X", 3, 0), ("h", 1, 1), ("X", 3, 1), ("WO", 1),
    ("WI", 1), ("h", 0, 0), ("WI", 2), ("WI", 5), ("X", 2, 1), ("X", 1, 1), ("h", 0, 1), ("WI", 3),
    ("WI", 0), ("WO", 0), ("WO", 2), ("WI", 4), ("X", 0, 0), ("Z", 0), ("X", 0, 1), ("Z", 1),
)


def gelu_pair(pre):
    inner = root_two_pi * (pre + 0.044715 * pre * pre * pre)
    bent = jnp.tanh(inner)
    act = 0.5 * pre * (1.0 + bent)
    slope = 0.5 * (1.0 + bent) + 0.5 * pre * (1.0 - bent * bent) * root_two_pi * (
        1.0 + 3.0 * 0.044715 * pre * pre
    )
    return act, slope


def kernel(
    tokens, grad_out, weight_in, weight_out,
    output, grad_in, grad_w_in, grad_w_out,
    panel, w_in, w_out, part, y_join, y_recv, z_send, z_recv, slope, hidden,
    o_part, o_recv, x_send, x_join, x_recv, e_send, e_recv, load_sem,
    az_rs, az_ss, ax_rs, ax_ss, sib_rs, sib_ss,
    y_rs, y_ss, z_rs, z_ss, hy_rs, hy_ss,
    o_rs, o_ss, x_rs, x_ss, e_rs, e_ss,
):
    row, col = lax.axis_index("row"), lax.axis_index("col")
    y, low = lax.rem(row, 4), lax.div(row, 4)
    core, x, z = lax.rem(col, 2), lax.rem(lax.div(col, 2), 4), lax.div(col, 8)

    def around(place, step):
        return lax.rem(place + step, 4)

    sibling = (row, z * 8 + x * 2 + (1 - core))
    partner = ((1 - low) * 4 + y, col)
    x_peer = {d: (row, z * 8 + around(x, d) * 2 + core) for d in AWAY}
    z_peer = {d: (row, around(z, d) * 8 + x * 2 + core) for d in AWAY}
    y_peer = {d: (low * 4 + around(y, d), col) for d in AWAY}
    sends = []

    def send(src, dst, send_sem, recv_sem, device):
        copy = pltpu.make_async_remote_copy(
            src_ref=src, dst_ref=dst, send_sem=send_sem, recv_sem=recv_sem,
            device_id=device, device_id_type=pl.DeviceIdType.MESH,
        )
        copy.start()
        sends.append(copy)

    def arrived(dst, send_sem, recv_sem):
        pltpu.make_async_remote_copy(
            src_ref=dst, dst_ref=dst, send_sem=send_sem, recv_sem=recv_sem,
            device_id=sibling, device_id_type=pl.DeviceIdType.MESH,
        ).wait_recv()

    loads = [
        pltpu.make_async_copy(tokens, panel.at[0, z, core, x], load_sem.at[0]),
        pltpu.make_async_copy(grad_out, panel.at[1, z, core, x], load_sem.at[1]),
        pltpu.make_async_copy(weight_in, w_in, load_sem.at[2]),
        pltpu.make_async_copy(weight_out, w_out, load_sem.at[3]),
    ]
    for load in loads:
        load.start()
    peers = [sibling, partner] + [p[d] for p in (x_peer, z_peer, y_peer) for d in AWAY]
    barrier = pltpu.get_barrier_semaphore()
    for peer in peers:
        pl.semaphore_signal(barrier, inc=1, device_id=peer, device_id_type=pl.DeviceIdType.MESH)
    pl.semaphore_wait(barrier, len(peers))

    def block(a, dx, dz, c):
        return panel.at[a, around(z, dz), c, around(x, dx)]

    def to_sibling(a, dx, dz):
        mine = block(a, dx, dz, core)
        send(mine, mine, sib_ss.at[a, dx, dz], sib_rs.at[a, dx, dz], sibling)

    def along_x(a, dz):
        mine = block(a, 0, dz, core)
        for d in AWAY[:2] if (a, dz) in RELAY_X else AWAY:
            send(mine, mine, ax_ss.at[a, d, dz], ax_rs.at[a, 4 - d, dz], x_peer[d])

    def gather_own(a):
        loads[a].wait()
        along_x(a, 0)
        mine = block(a, 0, 0, core)
        for d in AWAY[:2] if a in RELAY_Z else AWAY:
            send(mine, mine, az_ss.at[a, d], az_rs.at[a, 4 - d], z_peer[d])
        to_sibling(a, 0, 0)

    def gather_z(a, dz):
        arrived(block(a, 0, dz, core), az_ss.at[a, dz], az_rs.at[a, dz])
        along_x(a, dz)
        if a in RELAY_Z and dz == BACK[a]:
            mine = block(a, 0, dz, core)
            send(mine, mine, az_ss.at[a, 2], az_rs.at[a, 2], z_peer[ON[a]])
        to_sibling(a, 0, dz)

    def gather_x(a, dx, dz):
        arrived(block(a, dx, dz, core), ax_ss.at[a, dx, dz], ax_rs.at[a, dx, dz])
        if (a, dz) in RELAY_X and dx == BACK[a]:
            mine = block(a, dx, dz, core)
            send(mine, mine, ax_ss.at[a, 2, dz], ax_rs.at[a, 2, dz], x_peer[ON[a]])
        to_sibling(a, dx, dz)

    ready = set()

    def first(i, a):
        dz = CHUNKS[i]
        zk = around(z, dz)
        for dx in range(4):
            arrived(block(a, dx, dz, 1 - core), sib_ss.at[a, dx, dz], sib_rs.at[a, dx, dz])
        if a not in ready:
            ready.add(a)
            loads[2 + a].wait()

        @pl.loop(0, 768 // TILE_C)
        def _(n):
            cols = pl.ds(pl.multiple_of(n * TILE_C, TILE_C), TILE_C)
            left = panel[a, zk].reshape(128, 1536)
            if a == 0:
                total = jnp.dot(left, w_in[:, cols], preferred_element_type=F32)
            else:
                total = lax.dot_general(left, w_out[cols, :], NT, preferred_element_type=F32)
            part[i, a, :, :, :, cols] = total.astype(BF).reshape(4, 2, 16, TILE_C)

        def to_y(d, slot, device):
            send(
                part.at[i, a, around(y, d)], y_recv.at[i, a, slot],
                y_ss.at[i, a, slot], y_rs.at[i, a, slot], y_peer[device],
            )

        if (i, a) in RELAY_Y_SUM:
            to_y(2, 0, ON[a])
            to_y(BACK[a], 1, BACK[a])
        else:
            for d in AWAY:
                to_y(d, 3 - d, d)

    def y_arrived(i, a, slot):
        arrived(y_recv.at[i, a, slot], y_ss.at[i, a, slot], y_rs.at[i, a, slot])

    def join_y(i, a):
        y_arrived(i, a, 0)
        total = part[i, a, around(y, ON[a])].astype(F32) + y_recv[i, a, 0].astype(F32)
        y_join[i, a] = total.astype(BF)
        send(
            y_join.at[i, a], y_recv.at[i, a, 2],
            y_ss.at[i, a, 2], y_rs.at[i, a, 2], y_peer[ON[a]],
        )

    def sum_y(i, a):
        slots = (1, 2) if (i, a) in RELAY_Y_SUM else (0, 1, 2)
        total = part[i, a, y].astype(F32)
        for slot in slots:
            y_arrived(i, a, slot)
        for slot in slots:
            total = total + y_recv[i, a, slot].astype(F32)
        z_send[i, a] = total.astype(BF)
        send(z_send.at[i, a], z_recv.at[i, a], z_ss.at[i, a], z_rs.at[i, a], partner)

    def bend(i, a):
        zk = around(z, CHUNKS[i])
        arrived(z_recv.at[i, a], z_ss.at[i, a], z_rs.at[i, a])
        total = z_send[i, a].astype(F32) + z_recv[i, a].astype(F32)
        if a == 0:
            act, bent = gelu_pair(total)
            slope[i] = bent
            hidden[a, zk, y] = act.astype(BF)
        else:
            hidden[a, zk, y] = (total * slope[i]).astype(BF)
        both = hidden.at[a, zk, y]
        for d in AWAY[:2] if (i, a) in RELAY_Y else AWAY:
            send(both, both, hy_ss.at[i, a, d - 1], hy_rs.at[i, a, 3 - d], y_peer[d])

    def hidden_arrived(i, a, d):
        both = hidden.at[a, around(z, CHUNKS[i]), around(y, d)]
        arrived(both, hy_ss.at[i, a, d - 1], hy_rs.at[i, a, d - 1])
        return both

    def pass_on(i, a):
        both = hidden_arrived(i, a, BACK[a])
        send(both, both, hy_ss.at[i, a, 1], hy_rs.at[i, a, 1], y_peer[ON[a]])

    def second(i, a):
        zk = around(z, CHUNKS[i])
        for d in (ON[a], 2) if (i, a) in RELAY_Y else AWAY:
            hidden_arrived(i, a, d)

        @pl.loop(0, 1536 // TILE_G)
        def _(n):
            cols = pl.ds(pl.multiple_of(n * TILE_G, TILE_G), TILE_G)
            left = hidden[a, zk].reshape(128, 768)
            if a == 0:
                total = jnp.dot(left, w_out[:, cols], preferred_element_type=F32)
            else:
                total = lax.dot_general(left, w_in[cols, :], NT, preferred_element_type=F32)
            o_part[i, a, :, :, :, cols] = total.astype(BF).reshape(2, 4, 16, TILE_G)

        send(
            o_part.at[i, a, 1 - core], o_recv.at[i, a], o_ss.at[i, a], o_rs.at[i, a], sibling
        )

    def to_x(i, a, src, slot, device):
        send(
            src, x_recv.at[i, a, slot], x_ss.at[i, a, slot], x_rs.at[i, a, slot], x_peer[device]
        )

    def x_arrived(i, a, slot):
        arrived(x_recv.at[i, a, slot], x_ss.at[i, a, slot], x_rs.at[i, a, slot])

    def sum_core(i, a):
        arrived(o_recv.at[i, a], o_ss.at[i, a], o_rs.at[i, a])
        relay = (i, a) in RELAY_X_SUM
        for d in (2, BACK[a], ON[a], 0):
            xk = around(x, d)
            total = o_part[i, a, core, xk].astype(F32) + o_recv[i, a, xk].astype(F32)
            x_send[i, a, d] = total.astype(BF)
            if relay and d == 2:
                to_x(i, a, x_send.at[i, a, d], 0, ON[a])
            elif relay and d == BACK[a]:
                to_x(i, a, x_send.at[i, a, d], 1, d)
            elif not relay and d > 0:
                to_x(i, a, x_send.at[i, a, d], 3 - d, d)

    def join_x(i, a):
        x_arrived(i, a, 0)
        total = x_send[i, a, ON[a]].astype(F32) + x_recv[i, a, 0].astype(F32)
        x_join[i, a] = total.astype(BF)
        to_x(i, a, x_join.at[i, a], 2, ON[a])

    def sum_x(i, a):
        slots = (1, 2) if (i, a) in RELAY_X_SUM else (0, 1, 2)
        for slot in slots:
            x_arrived(i, a, slot)
        total = x_send[i, a, 0].astype(F32)
        for slot in slots:
            total = total + x_recv[i, a, slot].astype(F32)
        e_send[i, a] = total.astype(BF)
        dz = CHUNKS[i]
        if dz > 0:
            send(
                e_send.at[i, a], e_recv.at[a, 3 - dz],
                e_ss.at[a, dz - 1], e_rs.at[a, 3 - dz], z_peer[dz],
            )

    def sum_z(a):
        for d in AWAY:
            arrived(e_recv.at[a, d - 1], e_ss.at[a, d - 1], e_rs.at[a, d - 1])
        total = e_send[CHUNKS.index(0), a].astype(F32)
        for j in range(3):
            total = total + e_recv[a, j].astype(F32)
        (output, grad_in)[a][...] = total.astype(BF)

    factor = 1.0 / math.sqrt(512)

    def weight_in_grad(m):
        cols = pl.ds(m * TILE, TILE)
        left = panel[0, :, :, :, :, cols].reshape(512, TILE)
        grad = lax.dot_general(left, hidden[1].reshape(512, 768), TN, preferred_element_type=F32)
        grad_w_in[cols, :] = (grad * factor).astype(BF)

    def weight_out_grad(m):
        cols = pl.ds(m * TILE, TILE)
        left = hidden[0, :, :, :, :, cols].reshape(512, TILE)
        grad = lax.dot_general(left, panel[1].reshape(512, 1536), TN, preferred_element_type=F32)
        grad_w_out[cols, :] = (grad * factor).astype(BF)

    does = {
        "A0": gather_own, "A1": gather_z, "A2": gather_x, "c": first, "s": sum_y, "b": bend,
        "r": join_y, "f": pass_on, "g": second, "h": sum_core, "q": join_x, "X": sum_x, "Z": sum_z,
        "WI": weight_in_grad, "WO": weight_out_grad,
    }
    for name, *where in STEPS:
        does[name](*where)
    for copy in sends:
        copy.wait_send()


def write_out(*refs):
    n = len(refs) // 2
    copies = [pltpu.make_async_copy(refs[j], refs[n + j], refs[-1].at[j]) for j in range(n)]
    for copy in copies:
        copy.start()
    for copy in copies:
        copy.wait()


def shards(tokens, grad_out, weight_in, weight_out):
    dma = pltpu.SemaphoreType.DMA
    vmem = pltpu.VMEM
    like = jax.ShapeDtypeStruct
    shapes = (
        like(tokens.shape, BF), like(tokens.shape, BF),
        like(weight_in.shape, BF), like(weight_out.shape, BF),
    )
    tokens, grad_out = (
        pltpu.with_memory_space_constraint(arg, pltpu.HBM) for arg in (tokens, grad_out)
    )
    results = pl.pallas_call(
        kernel,
        out_shape=shapes,
        in_specs=[pl.BlockSpec(memory_space=IN_SPACE)] * 4,
        out_specs=[pl.BlockSpec(memory_space=OUT_SPACE)] * 4,
        scratch_shapes=[
            vmem((2, 4, 2, 4, 16, 1536), BF),
            vmem((1536, 768), BF),
            vmem((768, 1536), BF),
            vmem((4, 2, 4, 2, 16, 768), BF),
            vmem((4, 2, 2, 16, 768), BF),
            vmem((4, 2, 3, 2, 16, 768), BF),
            vmem((4, 2, 2, 16, 768), BF),
            vmem((4, 2, 2, 16, 768), BF),
            vmem((4, 2, 16, 768), F32),
            vmem((2, 4, 4, 2, 16, 768), BF),
            vmem((4, 2, 2, 4, 16, 1536), BF),
            vmem((4, 2, 4, 16, 1536), BF),
            vmem((4, 2, 4, 16, 1536), BF),
            vmem((4, 2, 16, 1536), BF),
            vmem((4, 2, 3, 16, 1536), BF),
            vmem((4, 2, 16, 1536), BF),
            vmem((2, 3, 16, 1536), BF),
            dma((4,)),
            dma((2, 4)), dma((2, 4)), dma((2, 4, 4)), dma((2, 4, 4)), dma((2, 4, 4)), dma((2, 4, 4)),
            dma((4, 2, 3)), dma((4, 2, 3)), dma((4, 2)), dma((4, 2)), dma((4, 2, 3)), dma((4, 2, 3)),
            dma((4, 2)), dma((4, 2)), dma((4, 2, 3)), dma((4, 2, 3)), dma((2, 3)), dma((2, 3)),
        ],
        compiler_params=pltpu.CompilerParams(
            collective_id=0, has_side_effects=True, vmem_limit_bytes=VMEM_LIMIT
        ),
        name="block",
    )(tokens, grad_out, weight_in, weight_out)
    return pl.pallas_call(
        write_out,
        out_shape=shapes,
        in_specs=[pl.BlockSpec(memory_space=MID_SPACE)] * 4,
        out_specs=[pl.BlockSpec(memory_space=pl.ANY)] * 4,
        scratch_shapes=[dma((4,))],
        compiler_params=pltpu.CompilerParams(vmem_limit_bytes=2**20),
        name="write_out",
    )(*results)


IN_SPACE = pltpu.HBM
OUT_SPACE = pltpu.VMEM
MID_SPACE = pltpu.VMEM
VMEM_LIMIT = 48 * 2**20


def solution(mesh):
    placed = (P("col", "row"), P("col", "row"), P("row", "col"), P("col", "row"))
    return jax.shard_map(
        shards, mesh=mesh, in_specs=placed, out_specs=placed, check_vma=False
    )
```

```python
import math

import jax
import jax.numpy as jnp
from jax import lax
from jax.experimental import pallas as pl
from jax.experimental.pallas import tpu as pltpu
from jax.sharding import PartitionSpec as P

root_two_pi = math.sqrt(2.0 / math.pi)
BF = jnp.bfloat16
F32 = jnp.float32
NT = (((1,), (1,)), ((), ()))
TN = (((0,), (0,)), ((), ()))
AWAY = (1, 3, 2)
TILE = 256
TILE_C = 768
TILE_G = 1536
CHUNKS = (0, 1, 3, 2)
RELAY_X = ()
RELAY_Z = ()
RELAY_Y_SUM = ()
RELAY_Y = ()
RELAY_X_SUM = ()
ON, BACK = (1, 3), (3, 1)
STEPS = (
    ("A0", 0), ("A0", 1), ("A2", 0, 3, 0), ("A2", 0, 1, 0), ("A1", 0, 3), ("A2", 0, 2, 0),
    ("A2", 1, 3, 0), ("A1", 0, 1), ("c", 0, 0), ("A2", 1, 1, 0), ("A2", 1, 2, 0), ("A2", 0, 1, 3),
    ("A2", 0, 3, 3), ("A1", 0, 2), ("c", 0, 1), ("A1", 1, 1), ("A2", 0, 2, 3), ("A2", 0, 3, 1),
    ("A2", 0, 1, 1), ("c", 2, 0), ("A2", 0, 2, 1), ("A1", 1, 2), ("A2", 0, 3, 2), ("A1", 1, 3),
    ("c", 1, 0), ("A2", 0, 1, 2), ("A2", 0, 2, 2), ("A2", 1, 1, 1), ("c", 3, 0), ("A2", 1, 3, 1),
    ("A2", 1, 2, 1), ("A2", 1, 1, 2), ("s", 2, 0), ("A2", 1, 3, 2), ("c", 1, 1), ("A2", 1, 2, 2),
    ("s", 1, 0), ("c", 3, 1), ("A2", 1, 2, 3), ("A2", 1, 3, 3), ("s", 3, 0), ("b", 2, 0),
    ("s", 0, 1), ("s", 0, 0), ("A2", 1, 1, 3), ("s", 1, 1), ("c", 2, 1), ("b", 3, 0), ("s", 3, 1),
    ("g", 2, 0), ("b", 1, 0), ("s", 2, 1), ("h", 2, 0), ("b", 1, 1), ("g", 3, 0), ("b", 3, 1),
    ("b", 2, 1), ("g", 1, 0), ("h", 3, 0), ("b", 0, 0), ("X", 2, 0), ("g", 1, 1), ("h", 1, 0),
    ("g", 3, 1), ("h", 1, 1), ("b", 0, 1), ("X", 3, 0), ("g", 2, 1), ("h", 3, 1), ("X", 1, 0),
    ("h", 2, 1), ("g", 0, 0), ("WO", 0), ("X", 1, 1), ("g", 0, 1), ("X", 3, 1), ("h", 0, 0),
    ("WI", 5), ("h", 0, 1), ("X", 2, 1), ("WI", 1), ("WI", 2), ("WI", 0), ("WO", 2), ("X", 0, 0),
    ("WO", 1), ("WI", 4), ("Z", 0), ("WI", 3), ("X", 0, 1), ("Z", 1),
)


def gelu_pair(pre):
    inner = root_two_pi * (pre + 0.044715 * pre * pre * pre)
    bent = jnp.tanh(inner)
    act = 0.5 * pre * (1.0 + bent)
    slope = 0.5 * (1.0 + bent) + 0.5 * pre * (1.0 - bent * bent) * root_two_pi * (
        1.0 + 3.0 * 0.044715 * pre * pre
    )
    return act, slope


def kernel(
    tokens, grad_out, weight_in, weight_out,
    output, grad_in, grad_w_in, grad_w_out,
    panel, w_in, w_out, part, y_join, y_recv, z_send, z_recv, slope, hidden,
    o_part, o_recv, x_send, x_join, x_recv, e_send, e_recv, load_sem,
    az_rs, az_ss, ax_rs, ax_ss, sib_rs, sib_ss,
    y_rs, y_ss, z_rs, z_ss, hy_rs, hy_ss,
    o_rs, o_ss, x_rs, x_ss, e_rs, e_ss,
):
    row, col = lax.axis_index("row"), lax.axis_index("col")
    y, low = lax.rem(row, 4), lax.div(row, 4)
    core, x, z = lax.rem(col, 2), lax.rem(lax.div(col, 2), 4), lax.div(col, 8)

    def around(place, step):
        return lax.rem(place + step, 4)

    sibling = (row, z * 8 + x * 2 + (1 - core))
    partner = ((1 - low) * 4 + y, col)
    x_peer = {d: (row, z * 8 + around(x, d) * 2 + core) for d in AWAY}
    z_peer = {d: (row, around(z, d) * 8 + x * 2 + core) for d in AWAY}
    y_peer = {d: (low * 4 + around(y, d), col) for d in AWAY}
    sends = []

    def send(src, dst, send_sem, recv_sem, device):
        copy = pltpu.make_async_remote_copy(
            src_ref=src, dst_ref=dst, send_sem=send_sem, recv_sem=recv_sem,
            device_id=device, device_id_type=pl.DeviceIdType.MESH,
        )
        copy.start()
        sends.append(copy)

    def arrived(dst, send_sem, recv_sem):
        pltpu.make_async_remote_copy(
            src_ref=dst, dst_ref=dst, send_sem=send_sem, recv_sem=recv_sem,
            device_id=sibling, device_id_type=pl.DeviceIdType.MESH,
        ).wait_recv()

    loads = [
        pltpu.make_async_copy(tokens, panel.at[0, z, core, x], load_sem.at[0]),
        pltpu.make_async_copy(grad_out, panel.at[1, z, core, x], load_sem.at[1]),
        pltpu.make_async_copy(weight_in, w_in, load_sem.at[2]),
        pltpu.make_async_copy(weight_out, w_out, load_sem.at[3]),
    ]
    for load in loads:
        load.start()
    peers = [sibling, partner] + [p[d] for p in (x_peer, z_peer, y_peer) for d in AWAY]
    barrier = pltpu.get_barrier_semaphore()
    for peer in peers:
        pl.semaphore_signal(barrier, inc=1, device_id=peer, device_id_type=pl.DeviceIdType.MESH)
    pl.semaphore_wait(barrier, len(peers))

    def block(a, dx, dz, c):
        return panel.at[a, around(z, dz), c, around(x, dx)]

    def to_sibling(a, dx, dz):
        mine = block(a, dx, dz, core)
        send(mine, mine, sib_ss.at[a, dx, dz], sib_rs.at[a, dx, dz], sibling)

    def along_x(a, dz):
        mine = block(a, 0, dz, core)
        for d in AWAY[:2] if (a, dz) in RELAY_X else AWAY:
            send(mine, mine, ax_ss.at[a, d, dz], ax_rs.at[a, 4 - d, dz], x_peer[d])

    def gather_own(a):
        loads[a].wait()
        mine = block(a, 0, 0, core)
        for d in AWAY[:2] if a in RELAY_Z else AWAY:
            send(mine, mine, az_ss.at[a, d], az_rs.at[a, 4 - d], z_peer[d])
        along_x(a, 0)
        to_sibling(a, 0, 0)

    def gather_z(a, dz):
        arrived(block(a, 0, dz, core), az_ss.at[a, dz], az_rs.at[a, dz])
        along_x(a, dz)
        if a in RELAY_Z and dz == BACK[a]:
            mine = block(a, 0, dz, core)
            send(mine, mine, az_ss.at[a, 2], az_rs.at[a, 2], z_peer[ON[a]])
        to_sibling(a, 0, dz)

    def gather_x(a, dx, dz):
        arrived(block(a, dx, dz, core), ax_ss.at[a, dx, dz], ax_rs.at[a, dx, dz])
        if (a, dz) in RELAY_X and dx == BACK[a]:
            mine = block(a, dx, dz, core)
            send(mine, mine, ax_ss.at[a, 2, dz], ax_rs.at[a, 2, dz], x_peer[ON[a]])
        to_sibling(a, dx, dz)

    ready = set()

    def first(i, a):
        dz = CHUNKS[i]
        zk = around(z, dz)
        for dx in range(4):
            arrived(block(a, dx, dz, 1 - core), sib_ss.at[a, dx, dz], sib_rs.at[a, dx, dz])
        if a not in ready:
            ready.add(a)
            loads[2 + a].wait()

        @pl.loop(0, 768 // TILE_C)
        def _(n):
            cols = pl.ds(pl.multiple_of(n * TILE_C, TILE_C), TILE_C)
            left = panel[a, zk].reshape(128, 1536)
            if a == 0:
                total = jnp.dot(left, w_in[:, cols], preferred_element_type=F32)
            else:
                total = lax.dot_general(left, w_out[cols, :], NT, preferred_element_type=F32)
            part[i, a, :, :, :, cols] = total.astype(BF).reshape(4, 2, 16, TILE_C)

        def to_y(d, slot, device):
            send(
                part.at[i, a, around(y, d)], y_recv.at[i, a, slot],
                y_ss.at[i, a, slot], y_rs.at[i, a, slot], y_peer[device],
            )

        if (i, a) in RELAY_Y_SUM:
            to_y(2, 0, ON[a])
            to_y(BACK[a], 1, BACK[a])
        else:
            for d in AWAY:
                to_y(d, 3 - d, d)

    def y_arrived(i, a, slot):
        arrived(y_recv.at[i, a, slot], y_ss.at[i, a, slot], y_rs.at[i, a, slot])

    def join_y(i, a):
        y_arrived(i, a, 0)
        total = part[i, a, around(y, ON[a])].astype(F32) + y_recv[i, a, 0].astype(F32)
        y_join[i, a] = total.astype(BF)
        send(
            y_join.at[i, a], y_recv.at[i, a, 2],
            y_ss.at[i, a, 2], y_rs.at[i, a, 2], y_peer[ON[a]],
        )

    def sum_y(i, a):
        slots = (1, 2) if (i, a) in RELAY_Y_SUM else (0, 1, 2)
        total = part[i, a, y].astype(F32)
        for slot in slots:
            y_arrived(i, a, slot)
        for slot in slots:
            total = total + y_recv[i, a, slot].astype(F32)
        z_send[i, a] = total.astype(BF)
        send(z_send.at[i, a], z_recv.at[i, a], z_ss.at[i, a], z_rs.at[i, a], partner)

    def bend(i, a):
        zk = around(z, CHUNKS[i])
        arrived(z_recv.at[i, a], z_ss.at[i, a], z_rs.at[i, a])
        total = z_send[i, a].astype(F32) + z_recv[i, a].astype(F32)
        if a == 0:
            act, bent = gelu_pair(total)
            slope[i] = bent
            hidden[a, zk, y] = act.astype(BF)
        else:
            hidden[a, zk, y] = (total * slope[i]).astype(BF)
        both = hidden.at[a, zk, y]
        for d in AWAY[:2] if (i, a) in RELAY_Y else AWAY:
            send(both, both, hy_ss.at[i, a, d - 1], hy_rs.at[i, a, 3 - d], y_peer[d])

    def hidden_arrived(i, a, d):
        both = hidden.at[a, around(z, CHUNKS[i]), around(y, d)]
        arrived(both, hy_ss.at[i, a, d - 1], hy_rs.at[i, a, d - 1])
        return both

    def pass_on(i, a):
        both = hidden_arrived(i, a, BACK[a])
        send(both, both, hy_ss.at[i, a, 1], hy_rs.at[i, a, 1], y_peer[ON[a]])

    def second(i, a):
        zk = around(z, CHUNKS[i])
        for d in (ON[a], 2) if (i, a) in RELAY_Y else AWAY:
            hidden_arrived(i, a, d)

        @pl.loop(0, 1536 // TILE_G)
        def _(n):
            cols = pl.ds(pl.multiple_of(n * TILE_G, TILE_G), TILE_G)
            left = hidden[a, zk].reshape(128, 768)
            if a == 0:
                total = jnp.dot(left, w_out[:, cols], preferred_element_type=F32)
            else:
                total = lax.dot_general(left, w_in[cols, :], NT, preferred_element_type=F32)
            o_part[i, a, :, :, :, cols] = total.astype(BF).reshape(2, 4, 16, TILE_G)

        send(
            o_part.at[i, a, 1 - core], o_recv.at[i, a], o_ss.at[i, a], o_rs.at[i, a], sibling
        )

    def to_x(i, a, src, slot, device):
        send(
            src, x_recv.at[i, a, slot], x_ss.at[i, a, slot], x_rs.at[i, a, slot], x_peer[device]
        )

    def x_arrived(i, a, slot):
        arrived(x_recv.at[i, a, slot], x_ss.at[i, a, slot], x_rs.at[i, a, slot])

    def sum_core(i, a):
        arrived(o_recv.at[i, a], o_ss.at[i, a], o_rs.at[i, a])
        relay = (i, a) in RELAY_X_SUM
        for d in (2, BACK[a], ON[a], 0):
            xk = around(x, d)
            total = o_part[i, a, core, xk].astype(F32) + o_recv[i, a, xk].astype(F32)
            x_send[i, a, d] = total.astype(BF)
            if relay and d == 2:
                to_x(i, a, x_send.at[i, a, d], 0, ON[a])
            elif relay and d == BACK[a]:
                to_x(i, a, x_send.at[i, a, d], 1, d)
            elif not relay and d > 0:
                to_x(i, a, x_send.at[i, a, d], 3 - d, d)

    def join_x(i, a):
        x_arrived(i, a, 0)
        total = x_send[i, a, ON[a]].astype(F32) + x_recv[i, a, 0].astype(F32)
        x_join[i, a] = total.astype(BF)
        to_x(i, a, x_join.at[i, a], 2, ON[a])

    def sum_x(i, a):
        slots = (1, 2) if (i, a) in RELAY_X_SUM else (0, 1, 2)
        for slot in slots:
            x_arrived(i, a, slot)
        total = x_send[i, a, 0].astype(F32)
        for slot in slots:
            total = total + x_recv[i, a, slot].astype(F32)
        e_send[i, a] = total.astype(BF)
        dz = CHUNKS[i]
        if dz > 0:
            send(
                e_send.at[i, a], e_recv.at[a, 3 - dz],
                e_ss.at[a, dz - 1], e_rs.at[a, 3 - dz], z_peer[dz],
            )

    def sum_z(a):
        for d in AWAY:
            arrived(e_recv.at[a, d - 1], e_ss.at[a, d - 1], e_rs.at[a, d - 1])
        total = e_send[CHUNKS.index(0), a].astype(F32)
        for j in range(3):
            total = total + e_recv[a, j].astype(F32)
        (output, grad_in)[a][...] = total.astype(BF)

    factor = 1.0 / math.sqrt(512)

    def weight_in_grad(m):
        cols = pl.ds(m * TILE, TILE)
        left = panel[0, :, :, :, :, cols].reshape(512, TILE)
        grad = lax.dot_general(left, hidden[1].reshape(512, 768), TN, preferred_element_type=F32)
        grad_w_in[cols, :] = (grad * factor).astype(BF)

    def weight_out_grad(m):
        cols = pl.ds(m * TILE, TILE)
        left = hidden[0, :, :, :, :, cols].reshape(512, TILE)
        grad = lax.dot_general(left, panel[1].reshape(512, 1536), TN, preferred_element_type=F32)
        grad_w_out[cols, :] = (grad * factor).astype(BF)

    does = {
        "A0": gather_own, "A1": gather_z, "A2": gather_x, "c": first, "s": sum_y, "b": bend,
        "r": join_y, "f": pass_on, "g": second, "h": sum_core, "q": join_x, "X": sum_x, "Z": sum_z,
        "WI": weight_in_grad, "WO": weight_out_grad,
    }
    for name, *where in STEPS:
        does[name](*where)
    for copy in sends:
        copy.wait_send()


def write_out(*refs):
    n = len(refs) // 2
    copies = [pltpu.make_async_copy(refs[j], refs[n + j], refs[-1].at[j]) for j in range(n)]
    for copy in copies:
        copy.start()
    for copy in copies:
        copy.wait()


def shards(tokens, grad_out, weight_in, weight_out):
    dma = pltpu.SemaphoreType.DMA
    vmem = pltpu.VMEM
    like = jax.ShapeDtypeStruct
    shapes = (
        like(tokens.shape, BF), like(tokens.shape, BF),
        like(weight_in.shape, BF), like(weight_out.shape, BF),
    )
    tokens, grad_out = (
        pltpu.with_memory_space_constraint(arg, pltpu.HBM) for arg in (tokens, grad_out)
    )
    results = pl.pallas_call(
        kernel,
        out_shape=shapes,
        in_specs=[pl.BlockSpec(memory_space=IN_SPACE)] * 4,
        out_specs=[pl.BlockSpec(memory_space=OUT_SPACE)] * 4,
        scratch_shapes=[
            vmem((2, 4, 2, 4, 16, 1536), BF),
            vmem((1536, 768), BF),
            vmem((768, 1536), BF),
            vmem((4, 2, 4, 2, 16, 768), BF),
            vmem((4, 2, 2, 16, 768), BF),
            vmem((4, 2, 3, 2, 16, 768), BF),
            vmem((4, 2, 2, 16, 768), BF),
            vmem((4, 2, 2, 16, 768), BF),
            vmem((4, 2, 16, 768), F32),
            vmem((2, 4, 4, 2, 16, 768), BF),
            vmem((4, 2, 2, 4, 16, 1536), BF),
            vmem((4, 2, 4, 16, 1536), BF),
            vmem((4, 2, 4, 16, 1536), BF),
            vmem((4, 2, 16, 1536), BF),
            vmem((4, 2, 3, 16, 1536), BF),
            vmem((4, 2, 16, 1536), BF),
            vmem((2, 3, 16, 1536), BF),
            dma((4,)),
            dma((2, 4)), dma((2, 4)), dma((2, 4, 4)), dma((2, 4, 4)), dma((2, 4, 4)), dma((2, 4, 4)),
            dma((4, 2, 3)), dma((4, 2, 3)), dma((4, 2)), dma((4, 2)), dma((4, 2, 3)), dma((4, 2, 3)),
            dma((4, 2)), dma((4, 2)), dma((4, 2, 3)), dma((4, 2, 3)), dma((2, 3)), dma((2, 3)),
        ],
        compiler_params=pltpu.CompilerParams(
            collective_id=0, has_side_effects=True, vmem_limit_bytes=VMEM_LIMIT
        ),
        name="block",
    )(tokens, grad_out, weight_in, weight_out)
    return pl.pallas_call(
        write_out,
        out_shape=shapes,
        in_specs=[pl.BlockSpec(memory_space=MID_SPACE)] * 4,
        out_specs=[pl.BlockSpec(memory_space=pl.ANY)] * 4,
        scratch_shapes=[dma((4,))],
        compiler_params=pltpu.CompilerParams(vmem_limit_bytes=2**20),
        name="write_out",
    )(*results)


IN_SPACE = pltpu.HBM
OUT_SPACE = pltpu.VMEM
MID_SPACE = pltpu.VMEM
VMEM_LIMIT = 48 * 2**20


def solution(mesh):
    placed = (P("col", "row"), P("col", "row"), P("row", "col"), P("col", "row"))
    return jax.shard_map(
        shards, mesh=mesh, in_specs=placed, out_specs=placed, check_vma=False
    )
```

```python
import math

import jax
import jax.numpy as jnp
from jax import lax
from jax.experimental import pallas as pl
from jax.experimental.pallas import tpu as pltpu
from jax.sharding import PartitionSpec as P

root_two_pi = math.sqrt(2.0 / math.pi)
BF = jnp.bfloat16
F32 = jnp.float32
NT = (((1,), (1,)), ((), ()))
TN = (((0,), (0,)), ((), ()))
AWAY = (1, 3, 2)
TILE = 256
LAG = 24
TILE_C = 768
TILE_G = 1536
CHUNKS = (0, 1, 3, 2)
RELAY_X = ()
RELAY_Z = ()
RELAY_Y_SUM = ()
RELAY_Y = ()
RELAY_X_SUM = ()
ON, BACK = (1, 3), (3, 1)
STEPS = (
    ("A0", 0), ("A0", 1), ("A2", 0, 3, 0), ("A2", 0, 1, 0), ("A1", 0, 3), ("A2", 0, 2, 0),
    ("A2", 1, 3, 0), ("A1", 0, 1), ("c", 0, 0), ("A2", 1, 1, 0), ("A2", 1, 2, 0), ("A2", 0, 1, 3),
    ("A2", 0, 3, 3), ("A1", 0, 2), ("c", 0, 1), ("A1", 1, 1), ("A2", 0, 2, 3), ("A2", 0, 3, 1),
    ("A2", 0, 1, 1), ("c", 2, 0), ("A2", 0, 2, 1), ("A1", 1, 2), ("A2", 0, 3, 2), ("A1", 1, 3),
    ("c", 1, 0), ("A2", 0, 1, 2), ("A2", 0, 2, 2), ("A2", 1, 1, 1), ("c", 3, 0), ("A2", 1, 3, 1),
    ("A2", 1, 2, 1), ("A2", 1, 1, 2), ("s", 2, 0), ("A2", 1, 3, 2), ("c", 1, 1), ("A2", 1, 2, 2),
    ("s", 1, 0), ("c", 3, 1), ("A2", 1, 2, 3), ("A2", 1, 3, 3), ("s", 3, 0), ("b", 2, 0),
    ("s", 0, 1), ("s", 0, 0), ("A2", 1, 1, 3), ("s", 1, 1), ("c", 2, 1), ("b", 3, 0), ("s", 3, 1),
    ("g", 2, 0), ("b", 1, 0), ("s", 2, 1), ("h", 2, 0), ("b", 1, 1), ("g", 3, 0), ("b", 3, 1),
    ("b", 2, 1), ("g", 1, 0), ("h", 3, 0), ("b", 0, 0), ("X", 2, 0), ("g", 1, 1), ("h", 1, 0),
    ("g", 3, 1), ("h", 1, 1), ("b", 0, 1), ("X", 3, 0), ("g", 2, 1), ("h", 3, 1), ("X", 1, 0),
    ("h", 2, 1), ("g", 0, 0), ("WO", 0), ("X", 1, 1), ("g", 0, 1), ("X", 3, 1), ("h", 0, 0),
    ("WI", 5), ("h", 0, 1), ("X", 2, 1), ("WI", 1), ("WI", 2), ("WI", 0), ("WO", 2), ("X", 0, 0),
    ("WO", 1), ("WI", 4), ("Z", 0), ("WI", 3), ("X", 0, 1), ("Z", 1),
)


def gelu_pair(pre):
    inner = root_two_pi * (pre + 0.044715 * pre * pre * pre)
    bent = jnp.tanh(inner)
    act = 0.5 * pre * (1.0 + bent)
    slope = 0.5 * (1.0 + bent) + 0.5 * pre * (1.0 - bent * bent) * root_two_pi * (
        1.0 + 3.0 * 0.044715 * pre * pre
    )
    return act, slope


def kernel(
    tokens, grad_out, weight_in, weight_out,
    output, grad_in, grad_w_in, grad_w_out,
    panel, w_in, w_out, part, y_join, y_recv, z_send, z_recv, slope, hidden,
    o_part, o_recv, x_send, x_join, x_recv, e_send, e_recv, load_sem,
    az_rs, az_ss, ax_rs, ax_ss, sib_rs, sib_ss,
    y_rs, y_ss, z_rs, z_ss, hy_rs, hy_ss,
    o_rs, o_ss, x_rs, x_ss, e_rs, e_ss,
):
    row, col = lax.axis_index("row"), lax.axis_index("col")
    y, low = lax.rem(row, 4), lax.div(row, 4)
    core, x, z = lax.rem(col, 2), lax.rem(lax.div(col, 2), 4), lax.div(col, 8)

    def around(place, step):
        return lax.rem(place + step, 4)

    sibling = (row, z * 8 + x * 2 + (1 - core))
    partner = ((1 - low) * 4 + y, col)
    x_peer = {d: (row, z * 8 + around(x, d) * 2 + core) for d in AWAY}
    z_peer = {d: (row, around(z, d) * 8 + x * 2 + core) for d in AWAY}
    y_peer = {d: (low * 4 + around(y, d), col) for d in AWAY}
    sends = []

    def send(src, dst, send_sem, recv_sem, device):
        copy = pltpu.make_async_remote_copy(
            src_ref=src, dst_ref=dst, send_sem=send_sem, recv_sem=recv_sem,
            device_id=device, device_id_type=pl.DeviceIdType.MESH,
        )
        copy.start()
        sends.append(copy)

    def arrived(dst, send_sem, recv_sem):
        pltpu.make_async_remote_copy(
            src_ref=dst, dst_ref=dst, send_sem=send_sem, recv_sem=recv_sem,
            device_id=sibling, device_id_type=pl.DeviceIdType.MESH,
        ).wait_recv()

    loads = [
        pltpu.make_async_copy(tokens, panel.at[0, z, core, x], load_sem.at[0]),
        pltpu.make_async_copy(grad_out, panel.at[1, z, core, x], load_sem.at[1]),
        pltpu.make_async_copy(weight_in, w_in, load_sem.at[2]),
        pltpu.make_async_copy(weight_out, w_out, load_sem.at[3]),
    ]
    for load in loads:
        load.start()
    peers = [sibling, partner] + [p[d] for p in (x_peer, z_peer, y_peer) for d in AWAY]
    barrier = pltpu.get_barrier_semaphore()
    for peer in peers:
        pl.semaphore_signal(barrier, inc=1, device_id=peer, device_id_type=pl.DeviceIdType.MESH)
    pl.semaphore_wait(barrier, len(peers))

    def block(a, dx, dz, c):
        return panel.at[a, around(z, dz), c, around(x, dx)]

    def to_sibling(a, dx, dz):
        mine = block(a, dx, dz, core)
        send(mine, mine, sib_ss.at[a, dx, dz], sib_rs.at[a, dx, dz], sibling)

    def along_x(a, dz):
        mine = block(a, 0, dz, core)
        for d in AWAY[:2] if (a, dz) in RELAY_X else AWAY:
            send(mine, mine, ax_ss.at[a, d, dz], ax_rs.at[a, 4 - d, dz], x_peer[d])

    def gather_own(a):
        loads[a].wait()
        mine = block(a, 0, 0, core)
        for d in AWAY[:2] if a in RELAY_Z else AWAY:
            send(mine, mine, az_ss.at[a, d], az_rs.at[a, 4 - d], z_peer[d])
        along_x(a, 0)
        to_sibling(a, 0, 0)

    def gather_z(a, dz):
        arrived(block(a, 0, dz, core), az_ss.at[a, dz], az_rs.at[a, dz])
        along_x(a, dz)
        if a in RELAY_Z and dz == BACK[a]:
            mine = block(a, 0, dz, core)
            send(mine, mine, az_ss.at[a, 2], az_rs.at[a, 2], z_peer[ON[a]])
        to_sibling(a, 0, dz)

    def gather_x(a, dx, dz):
        arrived(block(a, dx, dz, core), ax_ss.at[a, dx, dz], ax_rs.at[a, dx, dz])
        if (a, dz) in RELAY_X and dx == BACK[a]:
            mine = block(a, dx, dz, core)
            send(mine, mine, ax_ss.at[a, 2, dz], ax_rs.at[a, 2, dz], x_peer[ON[a]])
        to_sibling(a, dx, dz)

    ready = set()

    def first(i, a):
        dz = CHUNKS[i]
        zk = around(z, dz)
        for dx in range(4):
            arrived(block(a, dx, dz, 1 - core), sib_ss.at[a, dx, dz], sib_rs.at[a, dx, dz])
        if a not in ready:
            ready.add(a)
            loads[2 + a].wait()

        @pl.loop(0, 768 // TILE_C)
        def _(n):
            cols = pl.ds(pl.multiple_of(n * TILE_C, TILE_C), TILE_C)
            left = panel[a, zk].reshape(128, 1536)
            if a == 0:
                total = jnp.dot(left, w_in[:, cols], preferred_element_type=F32)
            else:
                total = lax.dot_general(left, w_out[cols, :], NT, preferred_element_type=F32)
            part[i, a, :, :, :, cols] = total.astype(BF).reshape(4, 2, 16, TILE_C)

        def to_y(d, slot, device):
            send(
                part.at[i, a, around(y, d)], y_recv.at[i, a, slot],
                y_ss.at[i, a, slot], y_rs.at[i, a, slot], y_peer[device],
            )

        if (i, a) in RELAY_Y_SUM:
            to_y(2, 0, ON[a])
            to_y(BACK[a], 1, BACK[a])
        else:
            for d in AWAY:
                to_y(d, 3 - d, d)

    def y_arrived(i, a, slot):
        arrived(y_recv.at[i, a, slot], y_ss.at[i, a, slot], y_rs.at[i, a, slot])

    def join_y(i, a):
        y_arrived(i, a, 0)
        total = part[i, a, around(y, ON[a])].astype(F32) + y_recv[i, a, 0].astype(F32)
        y_join[i, a] = total.astype(BF)
        send(
            y_join.at[i, a], y_recv.at[i, a, 2],
            y_ss.at[i, a, 2], y_rs.at[i, a, 2], y_peer[ON[a]],
        )

    def sum_y(i, a):
        slots = (1, 2) if (i, a) in RELAY_Y_SUM else (0, 1, 2)
        total = part[i, a, y].astype(F32)
        for slot in slots:
            y_arrived(i, a, slot)
        for slot in slots:
            total = total + y_recv[i, a, slot].astype(F32)
        z_send[i, a] = total.astype(BF)
        send(z_send.at[i, a], z_recv.at[i, a], z_ss.at[i, a], z_rs.at[i, a], partner)

    def bend(i, a):
        zk = around(z, CHUNKS[i])
        arrived(z_recv.at[i, a], z_ss.at[i, a], z_rs.at[i, a])
        total = z_send[i, a].astype(F32) + z_recv[i, a].astype(F32)
        if a == 0:
            act, bent = gelu_pair(total)
            slope[i] = bent
            hidden[a, zk, y] = act.astype(BF)
        else:
            hidden[a, zk, y] = (total * slope[i]).astype(BF)
        both = hidden.at[a, zk, y]
        for d in AWAY[:2] if (i, a) in RELAY_Y else AWAY:
            send(both, both, hy_ss.at[i, a, d - 1], hy_rs.at[i, a, 3 - d], y_peer[d])

    def hidden_arrived(i, a, d):
        both = hidden.at[a, around(z, CHUNKS[i]), around(y, d)]
        arrived(both, hy_ss.at[i, a, d - 1], hy_rs.at[i, a, d - 1])
        return both

    def pass_on(i, a):
        both = hidden_arrived(i, a, BACK[a])
        send(both, both, hy_ss.at[i, a, 1], hy_rs.at[i, a, 1], y_peer[ON[a]])

    def second(i, a):
        zk = around(z, CHUNKS[i])
        for d in (ON[a], 2) if (i, a) in RELAY_Y else AWAY:
            hidden_arrived(i, a, d)

        @pl.loop(0, 1536 // TILE_G)
        def _(n):
            cols = pl.ds(pl.multiple_of(n * TILE_G, TILE_G), TILE_G)
            left = hidden[a, zk].reshape(128, 768)
            if a == 0:
                total = jnp.dot(left, w_out[:, cols], preferred_element_type=F32)
            else:
                total = lax.dot_general(left, w_in[cols, :], NT, preferred_element_type=F32)
            o_part[i, a, :, :, :, cols] = total.astype(BF).reshape(2, 4, 16, TILE_G)

        send(
            o_part.at[i, a, 1 - core], o_recv.at[i, a], o_ss.at[i, a], o_rs.at[i, a], sibling
        )

    def to_x(i, a, src, slot, device):
        send(
            src, x_recv.at[i, a, slot], x_ss.at[i, a, slot], x_rs.at[i, a, slot], x_peer[device]
        )

    def x_arrived(i, a, slot):
        arrived(x_recv.at[i, a, slot], x_ss.at[i, a, slot], x_rs.at[i, a, slot])

    def sum_core(i, a):
        arrived(o_recv.at[i, a], o_ss.at[i, a], o_rs.at[i, a])
        relay = (i, a) in RELAY_X_SUM
        for d in (2, BACK[a], ON[a], 0):
            xk = around(x, d)
            total = o_part[i, a, core, xk].astype(F32) + o_recv[i, a, xk].astype(F32)
            x_send[i, a, d] = total.astype(BF)
            if relay and d == 2:
                to_x(i, a, x_send.at[i, a, d], 0, ON[a])
            elif relay and d == BACK[a]:
                to_x(i, a, x_send.at[i, a, d], 1, d)
            elif not relay and d > 0:
                to_x(i, a, x_send.at[i, a, d], 3 - d, d)

    def join_x(i, a):
        x_arrived(i, a, 0)
        total = x_send[i, a, ON[a]].astype(F32) + x_recv[i, a, 0].astype(F32)
        x_join[i, a] = total.astype(BF)
        to_x(i, a, x_join.at[i, a], 2, ON[a])

    def sum_x(i, a):
        slots = (1, 2) if (i, a) in RELAY_X_SUM else (0, 1, 2)
        for slot in slots:
            x_arrived(i, a, slot)
        total = x_send[i, a, 0].astype(F32)
        for slot in slots:
            total = total + x_recv[i, a, slot].astype(F32)
        e_send[i, a] = total.astype(BF)
        dz = CHUNKS[i]
        if dz > 0:
            send(
                e_send.at[i, a], e_recv.at[a, 3 - dz],
                e_ss.at[a, dz - 1], e_rs.at[a, 3 - dz], z_peer[dz],
            )

    def sum_z(a):
        for d in AWAY:
            arrived(e_recv.at[a, d - 1], e_ss.at[a, d - 1], e_rs.at[a, d - 1])
        total = e_send[CHUNKS.index(0), a].astype(F32)
        for j in range(3):
            total = total + e_recv[a, j].astype(F32)
        (output, grad_in)[a][...] = total.astype(BF)

    factor = 1.0 / math.sqrt(512)

    def weight_in_grad(m):
        cols = pl.ds(m * TILE, TILE)
        left = panel[0, :, :, :, :, cols].reshape(512, TILE)
        grad = lax.dot_general(left, hidden[1].reshape(512, 768), TN, preferred_element_type=F32)
        grad_w_in[cols, :] = (grad * factor).astype(BF)

    def weight_out_grad(m):
        cols = pl.ds(m * TILE, TILE)
        left = hidden[0, :, :, :, :, cols].reshape(512, TILE)
        grad = lax.dot_general(left, panel[1].reshape(512, 1536), TN, preferred_element_type=F32)
        grad_w_out[cols, :] = (grad * factor).astype(BF)

    does = {
        "A0": gather_own, "A1": gather_z, "A2": gather_x, "c": first, "s": sum_y, "b": bend,
        "r": join_y, "f": pass_on, "g": second, "h": sum_core, "q": join_x, "X": sum_x, "Z": sum_z,
        "WI": weight_in_grad, "WO": weight_out_grad,
    }
    issued = []
    waited = 0
    for step, (name, *where) in enumerate(STEPS):
        does[name](*where)
        issued.append(len(sends))
        if step >= LAG:
            for copy in sends[waited : issued[step - LAG]]:
                copy.wait_send()
            waited = issued[step - LAG]
    for copy in sends[waited:]:
        copy.wait_send()


def write_out(*refs):
    n = len(refs) // 2
    copies = [pltpu.make_async_copy(refs[j], refs[n + j], refs[-1].at[j]) for j in range(n)]
    for copy in copies:
        copy.start()
    for copy in copies:
        copy.wait()


def shards(tokens, grad_out, weight_in, weight_out):
    dma = pltpu.SemaphoreType.DMA
    vmem = pltpu.VMEM
    like = jax.ShapeDtypeStruct
    shapes = (
        like(tokens.shape, BF), like(tokens.shape, BF),
        like(weight_in.shape, BF), like(weight_out.shape, BF),
    )
    tokens, grad_out = (
        pltpu.with_memory_space_constraint(arg, pltpu.HBM) for arg in (tokens, grad_out)
    )
    results = pl.pallas_call(
        kernel,
        out_shape=shapes,
        in_specs=[pl.BlockSpec(memory_space=IN_SPACE)] * 4,
        out_specs=[pl.BlockSpec(memory_space=OUT_SPACE)] * 4,
        scratch_shapes=[
            vmem((2, 4, 2, 4, 16, 1536), BF),
            vmem((1536, 768), BF),
            vmem((768, 1536), BF),
            vmem((4, 2, 4, 2, 16, 768), BF),
            vmem((4, 2, 2, 16, 768), BF),
            vmem((4, 2, 3, 2, 16, 768), BF),
            vmem((4, 2, 2, 16, 768), BF),
            vmem((4, 2, 2, 16, 768), BF),
            vmem((4, 2, 16, 768), F32),
            vmem((2, 4, 4, 2, 16, 768), BF),
            vmem((4, 2, 2, 4, 16, 1536), BF),
            vmem((4, 2, 4, 16, 1536), BF),
            vmem((4, 2, 4, 16, 1536), BF),
            vmem((4, 2, 16, 1536), BF),
            vmem((4, 2, 3, 16, 1536), BF),
            vmem((4, 2, 16, 1536), BF),
            vmem((2, 3, 16, 1536), BF),
            dma((4,)),
            dma((2, 4)), dma((2, 4)), dma((2, 4, 4)), dma((2, 4, 4)), dma((2, 4, 4)), dma((2, 4, 4)),
            dma((4, 2, 3)), dma((4, 2, 3)), dma((4, 2)), dma((4, 2)), dma((4, 2, 3)), dma((4, 2, 3)),
            dma((4, 2)), dma((4, 2)), dma((4, 2, 3)), dma((4, 2, 3)), dma((2, 3)), dma((2, 3)),
        ],
        compiler_params=pltpu.CompilerParams(
            collective_id=0, has_side_effects=True, vmem_limit_bytes=VMEM_LIMIT
        ),
        name="block",
    )(tokens, grad_out, weight_in, weight_out)
    return pl.pallas_call(
        write_out,
        out_shape=shapes,
        in_specs=[pl.BlockSpec(memory_space=MID_SPACE)] * 4,
        out_specs=[pl.BlockSpec(memory_space=pl.ANY)] * 4,
        scratch_shapes=[dma((4,))],
        compiler_params=pltpu.CompilerParams(vmem_limit_bytes=2**20),
        name="write_out",
    )(*results)


IN_SPACE = pltpu.HBM
OUT_SPACE = pltpu.VMEM
MID_SPACE = pltpu.VMEM
VMEM_LIMIT = 48 * 2**20


def solution(mesh):
    placed = (P("col", "row"), P("col", "row"), P("row", "col"), P("col", "row"))
    return jax.shard_map(
        shards, mesh=mesh, in_specs=placed, out_specs=placed, check_vma=False
    )
```
